256 devices in a mesh: seq: 32 (over x, z), head: 8 (over y, core).
Axes of the slice: x: 4, y: 4, z: 8, core: 2. Of those that a mesh axis runs over, the one named last changes fastest.
Arguments:
- attn_queries: bfloat16 [16384, 16, 128], P('seq', 'head'), may hold values from -20 to 20
- attn_keys: bfloat16 [16384, 16, 128], P('seq', 'head'), may hold values from -20 to 20
- attn_values: bfloat16 [16384, 16, 128], P('seq', 'head'), may hold values from -6 to 6
- attn_out_grad: bfloat16 [16384, 16, 128], P('seq', 'head'), may hold values from -6 to 6
- ssm_input: bfloat16 [16384, 8192], P('seq', 'head'), may hold values from -6 to 6
- log_decay: float32 [16384, 128], P('seq', 'head'), may hold values from -1 to 0
- b_proj: bfloat16 [16384, 128], P('seq'), may hold values from -0.5 to 0.5
- c_proj: bfloat16 [16384, 128], P('seq'), may hold values from -0.5 to 0.5
- ssm_out_grad: bfloat16 [16384, 8192], P('seq', 'head'), may hold values from -0.29882812 to 0.29882812
- global_owner: int32 [128, 4], replicated, may hold values from 0 to 31, all different within a row; in each aligned block of 4 rows (0 to 3, 4 to 7, ...) at most 2 rows name the same one
- global_offset: int32 [128, 4], replicated, may hold values from 0 to 3
- global_count: int32 [128], replicated, may hold values from 3 to 4
Outputs:
- query_grad: bfloat16 [16384, 16, 128], P('seq', 'head')
- key_grad: bfloat16 [16384, 16, 128], P('seq', 'head')
- value_grad: bfloat16 [16384, 16, 128], P('seq', 'head')
- input_grad: bfloat16 [16384, 8192], P('seq', 'head')
- decay_grad: float32 [16384, 128], P('seq', 'head')
- b_grad: float32 [16384, 128], P('seq')
- c_grad: float32 [16384, 128], P('seq')
The draws below stay inside these ranges and needn't reach their ends.
Inputs may be any that keep to these rules, and one draw needn't show every extreme that they name: `global_owner`: in every aligned block of 4 rows (the query blocks of one index of seq) no index is named by more than 2 rows, and the 4 entries of a row differ. Only the first global_count[q] entries of row q of global_owner and global_offset are listed.
All inputs are finite; a program needn't handle non-finite values.
Results may differ from the reference program's by a relative error of at most 0.017.
Values may be sent and summed in bfloat16 or wider, within the bound.
No kernel may reach another device: no remote copies, remote signals or barrier semaphores. Data moves between devices by JAX's collectives and lax.ppermute only.
A program may use at most 192 MiB of HBM per device.

```python
import math
import jax
import jax.numpy as jnp
import numpy as np
from jax import lax

HD = 128
SH_DEV = 16
HP = 64
NST = 128
BLK = 128
STRETCH = 128
SEG = 4
GLOB = 4
TOK_DEV = 512
AHEADS = 16
SHEADS = 128
SEQ_LEN = 16384
QB_DEV = 4
QBLOCKS = 128
CAP = 2
N_SEQ = 32
N_HEAD = 8


def draw_attn_queries(key, part):
    key = jax.random.fold_in(key, 31)
    own_rows = jnp.clip(jax.random.normal(key, (SEQ_LEN, AHEADS, HD), jnp.float32), -4.0, 4.0)
    return own_rows.astype(jnp.bfloat16)


def draw_attn_keys(key, part):
    key = jax.random.fold_in(key, 32)
    own_rows = jnp.clip(jax.random.normal(key, (SEQ_LEN, AHEADS, HD), jnp.float32), -4.0, 4.0)
    return own_rows.astype(jnp.bfloat16)


def draw_log_decay(key, part):
    key = jax.random.fold_in(key, 41)
    subkeys = jax.random.split(key, 7)
    slow_share = 0.5
    slow_heads = jax.random.bernoulli(subkeys[0], slow_share, (SHEADS,))
    slow_rate = 0.5 / SEQ_LEN * jax.random.uniform(subkeys[1], (SHEADS,), jnp.float32, 0.3, 1.0)
    fast_rate = jax.random.uniform(subkeys[2], (SHEADS,), jnp.float32, 1.0 / 50.0, 1.0 / 30.0)
    proportion_of_attention_channels = jnp.where(slow_heads, slow_rate, fast_rate)
    window_extent = jax.random.uniform(subkeys[3], (SEQ_LEN // TOK_DEV, 1, SHEADS), jnp.float32, 0.5, 1.5)
    window_extent = jnp.broadcast_to(window_extent, (SEQ_LEN // TOK_DEV, TOK_DEV, SHEADS)).reshape(SEQ_LEN, SHEADS)
    approximate_guess = jax.random.uniform(subkeys[4], (SEQ_LEN, SHEADS), jnp.float32, 0.5, 1.5)
    spots = jax.random.randint(subkeys[5], (3,), 0, SEQ_LEN)
    recurrence_steps_total = jax.random.uniform(subkeys[6], (3, 1), jnp.float32, 0.22, 0.4)
    matched_tally = (jnp.arange(SEQ_LEN)[None, :] == spots[:, None]).astype(jnp.float32)
    contiguous_tokens_per_block = jnp.sum(matched_tally * recurrence_steps_total, axis=0)[:, None]
    return -(proportion_of_attention_channels[None, :] * window_extent * approximate_guess + contiguous_tokens_per_block)


def touch_ends(entries, key, smallest, high):
    index_at = [jax.random.randint(jax.random.fold_in(key, axis), (), 0, length) for axis, length in enumerate(entries.shape)]
    longest = entries.shape.index(max(entries.shape))
    neighbour = index_at[:longest] + [(index_at[longest] + 1) % entries.shape[longest]] + index_at[longest + 1:]
    return entries.at[tuple(index_at)].set(smallest).at[tuple(neighbour)].set(high)


def block_scale(own_key, shape, shards, least, high):
    loudness, own = 1.0, jax.random.fold_in(own_key, 6)
    for axis_at, blocks in shards:
        draws = jnp.exp(jax.random.uniform(jax.random.fold_in(own, axis_at), (blocks,), jnp.float32, least / len(shards), high / len(shards)))
        loudness = loudness * jnp.repeat(draws, shape[axis_at] // blocks).reshape([-1 if axis == axis_at else 1 for axis in range(len(shape))])
    return loudness


def deal_out(stream_key, own, number, rows, number_of, top, most, slope):
    ranking = jax.random.permutation(stream_key, number_of)
    heavy_load, usual = shares(number_of, rows * top, most, slope, True), shares(number_of, rows * top, most, slope, False)
    places = jnp.arange(number_of)

    def named(tallies, offset_by):
        used = int((tallies > 0).sum())
        fixed = max(1, used // 4)
        moved = fixed + (places - fixed + offset_by * (used - fixed)) % max(1, number_of - fixed)
        return jnp.zeros((number_of,), jnp.int32).at[ranking[jnp.where(places < fixed, places, moved)]].set(jnp.asarray(tallies, jnp.int32))

    tallies = jnp.where(number % 4 == 0, named(heavy_load, number // 4), named(usual, number - number // 4 - 1))
    mixed = jax.random.permutation(jax.random.fold_in(own, 3), number_of)
    giver, taker = mixed[0:number_of // 2 * 2:2], mixed[1:number_of // 2 * 2:2]
    room = jnp.minimum(tallies[giver] - 1, most - tallies[taker]) // 2
    room = jnp.where((giver == ranking[0]) | (taker == ranking[0]) | (tallies[taker] == 0), 0, jnp.maximum(room, 0))
    moved = jax.random.randint(jax.random.fold_in(own, 4), (number_of // 2,), 0, 1 << 20) % (room + 1)
    tallies = tallies.at[giver].add(-moved).at[taker].add(moved)
    members = jnp.searchsorted(jnp.cumsum(tallies), jnp.arange(rows * top), side="right").astype(jnp.int32)
    grid = members.reshape(top, rows).T
    grid = grid[jax.random.permutation(jax.random.fold_in(own, 1), rows)]
    offset_by = jax.random.randint(jax.random.fold_in(own, 2), (rows, 1), 0, top)
    return jnp.take_along_axis(grid, (jnp.arange(top)[None, :] + offset_by) % top, axis=1)


def shares(amount, total, limit, skew, full):
    loads = [(1 << 20) // math.isqrt(rank ** skew) + 1 for rank in range(1, amount + 1)]
    largest = limit if full else min(limit, max(-(-total // amount), total * loads[0] // sum(loads)))
    least = 1 if total - largest >= amount - 1 else 0
    given, spare = [largest] + [least] * (amount - 1), total - largest - least * (amount - 1)
    while spare > 0:
        candidates = [i for i in range(1, amount) if given[i] < largest] or [i for i in range(1, amount) if given[i] < limit]
        pool, left = sum([loads[i] for i in candidates]), spare
        for i in candidates:
            more = min(limit - given[i], max(1, left * loads[i] // pool), spare)
            given[i] = given[i] + more
            spare = spare - more
    return np.array(given)


def normal_values(own_key, extent, width, bound, cuts=(), kind=jnp.bfloat16):
    level = block_scale(own_key, extent, cuts, -0.22, 0.18) if cuts else 1.0
    values = jax.random.normal(own_key, extent, jnp.float32) * width * level
    return jnp.minimum(jnp.maximum(values, -bound), bound).astype(kind)


def setup_inputs(seed: int = 0) -> dict:
    streams_of = jax.random.split(jax.random.key(seed), 13)
    attn_queries = draw_attn_queries(jax.random.fold_in(streams_of[12], 71), 0)
    attn_keys = draw_attn_keys(jax.random.fold_in(streams_of[12], 71), 0)
    attn_values = normal_values(streams_of[2], (SEQ_LEN, AHEADS, HD), 1.0, 6.0, ((0, 32), (1, 8)))
    attn_out_grad = normal_values(streams_of[3], (SEQ_LEN, AHEADS, HD), 1.0, 6.0, ((0, 32), (1, 8)))
    ssm_input = normal_values(streams_of[4], (SEQ_LEN, SHEADS * HP), 1.0, 6.0, ((0, 32), (1, 8)))
    log_decay = draw_log_decay(jax.random.fold_in(streams_of[12], 71), 0)
    b_proj = normal_values(streams_of[6], (SEQ_LEN, NST), NST ** -0.5, 0.5, ((0, 32),))
    c_proj = normal_values(streams_of[7], (SEQ_LEN, NST), NST ** -0.5, 0.5, ((0, 32),))
    ssm_out_grad = normal_values(streams_of[8], (SEQ_LEN, SHEADS * HP), 0.05, 0.29882812, ((0, 32), (1, 8)))
    global_owner_keys = jax.random.split(jax.random.fold_in(streams_of[9], 1), QBLOCKS // QB_DEV)
    global_owner_turns = jax.random.permutation(jax.random.fold_in(streams_of[9], 3), QBLOCKS // QB_DEV)
    global_owner = jax.vmap(lambda own, number: deal_out(jax.random.fold_in(streams_of[9], 2), own, number, QB_DEV, N_SEQ, GLOB, CAP, 2))(global_owner_keys, global_owner_turns).reshape((QBLOCKS, GLOB))
    global_offset = touch_ends(jax.random.randint(streams_of[10], (QBLOCKS, GLOB), 0, QB_DEV), jax.random.fold_in(streams_of[10], 1), 0, QB_DEV - 1).astype(jnp.int32)
    global_count = touch_ends(jax.random.randint(streams_of[11], (QBLOCKS,), GLOB - 1, GLOB + 1), jax.random.fold_in(streams_of[11], 1), GLOB - 1, GLOB).astype(jnp.int32)
    return dict(attn_queries=attn_queries, attn_keys=attn_keys, attn_values=attn_values, attn_out_grad=attn_out_grad, ssm_input=ssm_input, log_decay=log_decay, b_proj=b_proj, c_proj=c_proj, ssm_out_grad=ssm_out_grad, global_owner=global_owner, global_offset=global_offset, global_count=global_count)


HIGH = lax.Precision.HIGHEST

def ssd_output(x_rows, decay_log, b_rows, c_rows):
    head_count = decay_log.shape[1]
    stretch_count = x_rows.shape[0] // STRETCH
    x_stretches = x_rows.reshape(stretch_count, STRETCH, head_count, HP)
    l_stretches = decay_log.reshape(stretch_count, STRETCH, head_count)
    b_stretches = b_rows.reshape(stretch_count, STRETCH, NST)
    c_stretches = c_rows.reshape(stretch_count, STRETCH, NST)
    causal = (jnp.arange(STRETCH)[:, None] >= jnp.arange(STRETCH)[None, :])[:, :, None]

    def advance(state, inputs):
        x_stretch, l_stretch, b_stretch, c_stretch = inputs
        cumul = jnp.cumsum(l_stretch, axis=0)
        spread = cumul[:, None, :] - cumul[None, :, :]
        decays = jnp.where(causal, jnp.exp(jnp.where(causal, spread, 0.0)), 0.0)
        cb_inner = jnp.dot(c_stretch, b_stretch.T, precision=HIGH)
        weights = decays * cb_inner[:, :, None]
        output = jnp.einsum('ijh,jhp->ihp', weights, x_stretch, precision=HIGH)
        output = output + jnp.exp(cumul)[:, :, None] * jnp.einsum('hpn,in->ihp', state, c_stretch, precision=HIGH)
        tail_decay = jnp.exp(cumul[-1][None, :] - cumul)
        fresh = jnp.exp(cumul[-1])[:, None, None] * state + jnp.einsum('jhp,jn->hpn', tail_decay[:, :, None] * x_stretch, b_stretch, precision=HIGH)
        return (fresh, output)
    start = jnp.zeros((head_count, HP, NST), jnp.float32)
    _, outputs = lax.scan(advance, start, (x_stretches, l_stretches, b_stretches, c_stretches))
    return outputs.reshape(x_rows.shape[0], head_count, HP)

def ssd_grads(ssm_input, log_decay, b_proj, c_proj, ssm_out_grad):
    x_groups = ssm_input.astype(jnp.float32).reshape(SEQ_LEN, N_HEAD, SH_DEV, HP).transpose(1, 0, 2, 3)
    g_groups = ssm_out_grad.astype(jnp.float32).reshape(SEQ_LEN, N_HEAD, SH_DEV, HP).transpose(1, 0, 2, 3)
    l_groups = log_decay.reshape(SEQ_LEN, N_HEAD, SH_DEV).transpose(1, 0, 2)
    b_rows = b_proj.astype(jnp.float32)
    c_rows = c_proj.astype(jnp.float32)

    def one_group(inputs):
        x_group, l_group, g_group = inputs
        _, pullback = jax.vjp(ssd_output, x_group, l_group, b_rows, c_rows)
        return pullback(g_group)
    x_grads, l_grads, b_grads, c_grads = lax.map(one_group, (x_groups, l_groups, g_groups))
    input_grad = x_grads.transpose(1, 0, 2, 3).reshape(SEQ_LEN, SHEADS * HP).astype(jnp.bfloat16)
    decay_grad = l_grads.transpose(1, 0, 2).reshape(SEQ_LEN, SHEADS)
    return (input_grad, decay_grad, lax.optimization_barrier(jnp.sum(b_grads, axis=0)), lax.optimization_barrier(jnp.sum(c_grads, axis=0)))

def attention_head(inputs, target, valid):
    query_rows, key_rows, value_rows, grad_rows = inputs
    score_scale = 1.0 / math.sqrt(HD)
    seg_count = QBLOCKS // SEG
    seg_span = SEG * BLK
    query_blocks = query_rows.reshape(QBLOCKS, BLK, HD).astype(jnp.float32)
    grad_blocks = grad_rows.reshape(QBLOCKS, BLK, HD).astype(jnp.float32)

    def listed(rows):
        row_blocks = rows.reshape(QBLOCKS, BLK, HD)
        near_part = jnp.broadcast_to(rows.reshape(seg_count, 1, seg_span, HD), (seg_count, SEG, seg_span, HD)).reshape(QBLOCKS, seg_span, HD)
        remote = jnp.take(row_blocks, target.reshape(-1), axis=0).reshape(QBLOCKS, GLOB * BLK, HD)
        return jnp.concatenate([near_part, remote], axis=1).astype(jnp.float32)
    key_list = listed(key_rows)
    value_list = listed(value_rows)
    key_keep = jnp.concatenate([jnp.ones((QBLOCKS, seg_span), jnp.bool_), jnp.repeat(valid, BLK, axis=1)], axis=1)[:, None, :]
    scores = jnp.einsum('qid,qjd->qij', query_blocks, key_list) * score_scale
    scores = jnp.where(key_keep, scores, -jnp.inf)
    highest = lax.optimization_barrier(jnp.max(scores, axis=-1, keepdims=True))
    exp_scores = jnp.where(key_keep, jnp.exp(scores - highest), 0.0)
    weights_f = exp_scores / lax.optimization_barrier(jnp.sum(exp_scores, axis=-1, keepdims=True))
    weights_b = lax.optimization_barrier(weights_f.astype(jnp.bfloat16)).astype(jnp.float32)
    attn_out = jnp.einsum('qij,qjd->qid', weights_b, value_list)
    row_delta = lax.optimization_barrier(jnp.sum(grad_blocks * attn_out, axis=-1))
    dprob = jnp.einsum('qid,qjd->qij', grad_blocks, value_list)
    dscore = (weights_f * (dprob - row_delta[:, :, None]) * score_scale).astype(jnp.bfloat16)
    dscore = lax.optimization_barrier(dscore).astype(jnp.float32)
    q_grad = jnp.einsum('qij,qjd->qid', dscore, key_list)
    k_part = jnp.einsum('qij,qid->qjd', dscore, query_blocks)
    v_part = jnp.einsum('qij,qid->qjd', weights_b, grad_blocks)
    target_ids = jnp.where(valid, target, QBLOCKS).reshape(-1)

    def settle(partial_rows):
        near_sum = partial_rows[:, :seg_span].reshape(seg_count, SEG, seg_span, HD).sum(axis=1).reshape(QBLOCKS, BLK, HD)
        remote = partial_rows[:, seg_span:].reshape(QBLOCKS * GLOB, BLK, HD).astype(jnp.bfloat16)
        remote = lax.optimization_barrier(remote).astype(jnp.float32)
        summed = jax.ops.segment_sum(remote, target_ids, num_segments=QBLOCKS + 1)[:QBLOCKS]
        return (near_sum + summed).reshape(SEQ_LEN, HD).astype(jnp.bfloat16)
    return (q_grad.reshape(SEQ_LEN, HD).astype(jnp.bfloat16), settle(k_part), settle(v_part))

def reference(attn_queries, attn_keys, attn_values, attn_out_grad, ssm_input, log_decay, b_proj, c_proj, ssm_out_grad, global_owner, global_offset, global_count):
    target = (global_owner * QB_DEV + global_offset).astype(jnp.int32)
    valid = jnp.arange(GLOB)[None, :] < global_count[:, None]

    def per_head(inputs):
        return attention_head(inputs, target, valid)
    stacks = tuple((tensor.transpose(1, 0, 2) for tensor in (attn_queries, attn_keys, attn_values, attn_out_grad)))
    q_grads, k_grads, v_grads = lax.map(per_head, stacks)
    query_grad = q_grads.transpose(1, 0, 2)
    key_grad = k_grads.transpose(1, 0, 2)
    value_grad = v_grads.transpose(1, 0, 2)
    input_grad, decay_grad, b_grad, c_grad = ssd_grads(ssm_input, log_decay, b_proj, c_proj, ssm_out_grad)
    return (query_grad, key_grad, value_grad, input_grad, decay_grad, b_grad, c_grad)
```

```python
import functools
import math

import jax
import jax.numpy as jnp
from jax import lax
from jax.experimental import pallas as pl
from jax.experimental.pallas import tpu as pltpu
from jax.sharding import PartitionSpec as P

HD = 128
HP = 64
NST = 128
BLK = 128
STRETCH = 128
SEG = 4
GLOB = 4
TOK = 512
SH = 16
WIDTH = SH * HP
ITEMS = SEG * GLOB
NX = 4
NZ = 8
NS = NX * NZ
ROWS = WIDTH // NS
PAY = 2 * ROWS + 16
FAST = 8
STRETCHES = TOK // STRETCH

HIGH = lax.Precision.HIGHEST
F32 = jnp.float32
BF16 = jnp.bfloat16
Z_GROUPS = [[x * NZ + z for z in range(NZ)] for x in range(NX)]
X_GROUPS = [[x * NZ + z for x in range(NX)] for z in range(NZ)]


def dot(a, b, dims, precision=None):
    return lax.dot_general(
        a, b, (dims, ((), ())), precision=precision, preferred_element_type=F32
    )


def mm(a, b):
    return dot(a, b, ((1,), (0,)))


def mm_nt(a, b):
    return dot(a, b, ((1,), (1,)))


def mm_tn(a, b):
    return dot(a, b, ((0,), (0,)))


def call(body, name, outs, ins, scratch, flops, nbytes, vmem=48 << 20):
    return pl.pallas_call(
        body,
        out_shape=[jax.ShapeDtypeStruct(s, d) for s, d, _ in outs],
        in_specs=[pl.BlockSpec(memory_space=m) for m in ins],
        out_specs=[pl.BlockSpec(memory_space=m) for _, _, m in outs],
        scratch_shapes=scratch,
        compiler_params=pltpu.CompilerParams(vmem_limit_bytes=vmem),
        cost_estimate=pl.CostEstimate(flops=flops, bytes_accessed=nbytes, transcendentals=0),
        name=name,
    )


def gather_body(cap, codes, me, column, out, sem):
    here = me[0]
    my_x = here >> 3
    my_z = here & 7

    for x in range(NX):
        base = (x * NZ + my_z) * ITEMS

        def step(i, used, x=x, base=base):
            code = codes[base + i]
            hit = (code >= 0) & ((code >> 5) == my_x)

            @pl.when(hit)
            def _():
                block = code & 31
                pltpu.make_async_copy(
                    column.at[block >> 2, :, pl.ds((block & 3) * BLK, BLK), :],
                    out.at[x, used],
                    sem,
                ).start()

            return used + hit.astype(jnp.int32)

        used = lax.fori_loop(0, ITEMS, step, jnp.int32(0))

        def fill(c, _, x=x):
            pltpu.make_async_copy(
                column.at[0, :, pl.ds(0, BLK), :], out.at[x, c], sem
            ).start()
            return 0

        lax.fori_loop(used, cap, fill, 0)
    pltpu.make_async_copy(out, out, sem).wait()


def gather_blocks(cap, codes, me, column):
    return call(
        functools.partial(gather_body, cap),
        "pick_blocks",
        [((NX, cap, 2, BLK, HD), BF16, pl.ANY)],
        [pltpu.SMEM, pltpu.SMEM, pl.ANY],
        [pltpu.SemaphoreType.DMA],
        0,
        16 << 20,
    )(codes, me, column)[0]


def attend_body(
    cap, codes, me, q_ref, k_ref, v_ref, o_ref, far_in, dq_ref, near_ref, far_out,
    p_keep, s_keep, slots, counts,
):
    scale = 1.0 / math.sqrt(HD)
    base = me[0] * ITEMS
    for j in range(NX):
        counts[j] = 0

    def place(i, _):
        code = codes[base + i]
        live = code >= 0
        col = jnp.where(live, code >> 5, 0)
        rank = counts[col]
        slots[i] = jnp.where(live, col * cap + rank, -1)
        counts[col] = rank + live.astype(jnp.int32)
        return 0

    lax.fori_loop(0, ITEMS, place, 0)
    keys = k_ref[...]
    values = v_ref[...]
    for b in range(SEG):
        rows = pl.ds(b * BLK, BLK)
        q = q_ref[rows, :]
        o = o_ref[rows, :]
        scores = [mm_nt(q, keys) * scale]
        far_k = []
        far_v = []
        for g in range(GLOB):
            slot = slots[b * GLOB + g]
            at = jnp.maximum(slot, 0)
            far_k.append(far_in[at, 0])
            far_v.append(far_in[at, 1])
            raw = mm_nt(q, far_k[g]) * scale
            scores.append(jnp.where(slot >= 0, raw, -jnp.inf))
        high = functools.reduce(
            jnp.maximum, [jnp.max(s, axis=-1, keepdims=True) for s in scores]
        )
        exps = [jnp.exp(s - high) for s in scores]
        total = functools.reduce(jnp.add, [jnp.sum(e, axis=-1, keepdims=True) for e in exps])
        inv = 1.0 / total
        probs = [e * inv for e in exps]
        probs_b = [p.astype(BF16) for p in probs]
        dprob = [mm_nt(o, values)] + [mm_nt(o, v) for v in far_v]
        delta = functools.reduce(
            jnp.add,
            [jnp.sum(p.astype(F32) * d, axis=-1, keepdims=True) for p, d in zip(probs_b, dprob)],
        )
        dscore = [
            (p * (d - delta) * scale).astype(BF16) for p, d in zip(probs, dprob)
        ]
        dq = mm(dscore[0], keys)
        for g in range(GLOB):
            dq = dq + mm(dscore[g + 1], far_k[g])
        dq_ref[rows, :] = dq.astype(BF16)
        p_keep[rows, :] = probs_b[0]
        s_keep[rows, :] = dscore[0]
        for g in range(GLOB):
            slot = slots[b * GLOB + g]
            k_part = mm_tn(dscore[g + 1], q).astype(BF16)
            v_part = mm_tn(probs_b[g + 1], o).astype(BF16)

            @pl.when(slot >= 0)
            def _(slot=slot, k_part=k_part, v_part=v_part):
                far_out[slot, 0] = k_part
                far_out[slot, 1] = v_part

    near_ref[0] = mm_tn(s_keep[...], q_ref[...])
    near_ref[1] = mm_tn(p_keep[...], o_ref[...])


def attend(cap, codes, me, q, k, v, o, incoming):
    slots = NX * cap
    vm = pltpu.VMEM
    return call(
        functools.partial(attend_body, cap),
        "attend_head",
        [
            ((TOK, HD), BF16, vm),
            ((2, TOK, HD), F32, vm),
            ((slots, 2, BLK, HD), BF16, vm),
        ],
        [pltpu.SMEM, pltpu.SMEM] + [vm] * 5,
        [
            vm((TOK, TOK), BF16),
            vm((TOK, TOK), BF16),
            pltpu.SMEM((ITEMS,), jnp.int32),
            pltpu.SMEM((NX,), jnp.int32),
        ],
        5 * 2 * TOK * 1024 * HD * 4,
        8 << 20,
    )(codes, me, q, k, v, o, incoming.reshape(slots, 2, BLK, HD))


def combine_body(codes, me, back, out, total):
    here = me[0]
    my_x = here >> 3
    my_z = here & 7
    total[...] = jnp.zeros_like(total)
    for x in range(NX):
        base = (x * NZ + my_z) * ITEMS

        def step(i, used, x=x, base=base):
            code = codes[base + i]
            hit = (code >= 0) & ((code >> 5) == my_x)

            @pl.when(hit)
            def _():
                block = code & 31
                rows = pl.ds(pl.multiple_of((block & 3) * BLK, BLK), BLK)
                for s in range(2):
                    total[block >> 2, s, rows, :] += back[x, used, s].astype(F32)

            return used + hit.astype(jnp.int32)

        lax.fori_loop(0, ITEMS, step, jnp.int32(0))
    out[...] = total[...].astype(BF16)


def combine(codes, me, back):
    vm = pltpu.VMEM
    return call(
        combine_body,
        "sum_partials",
        [((NZ, 2, TOK, HD), BF16, vm)],
        [pltpu.SMEM, pltpu.SMEM, vm],
        [vm((NZ, 2, TOK, HD), F32)],
        0,
        8 << 20,
    )(codes, me, back)[0]


def triangle(lower):
    i = lax.broadcasted_iota(jnp.int32, (STRETCH, STRETCH), 0)
    j = lax.broadcasted_iota(jnp.int32, (STRETCH, STRETCH), 1)
    return i >= j if lower else i <= j


def head_map(transposed):
    shape = (WIDTH, SH) if transposed else (SH, WIDTH)
    wide = lax.broadcasted_iota(jnp.int32, shape, 0 if transposed else 1)
    head = lax.broadcasted_iota(jnp.int32, shape, 1 if transposed else 0)
    return ((wide >> 6) == head).astype(BF16)


def two_part(a, b):
    high = a.astype(BF16)
    low = (a - high.astype(F32)).astype(BF16)
    return mm(high, b) + mm(low, b)


def per_head(rates, state):
    return jnp.concatenate(
        [state[h * HP : (h + 1) * HP, :] * rates[0:1, h : h + 1] for h in range(SH)], axis=0
    )


def ends_body(x_ref, g_ref, ld_ref, b_ref, c_ref, ends, starts, pay):
    lower = triangle(True).astype(F32)
    spread = head_map(False)
    last = []
    for k in range(STRETCHES):
        rows = pl.ds(k * STRETCH, STRETCH)
        cumul = dot(lower, ld_ref[rows, :], ((1,), (0,)), HIGH)
        tot = cumul[STRETCH - 1 : STRETCH, :]
        last.append(tot)
        tail = two_part(jnp.exp(tot - cumul), spread)
        lead = two_part(jnp.exp(cumul), spread)
        x_in = (x_ref[rows, :].astype(F32) * tail).astype(BF16)
        g_in = (g_ref[rows, :].astype(F32) * lead).astype(BF16)
        ends[k] = mm_tn(x_in, b_ref[rows, :])
        starts[k] = mm_tn(g_in, c_ref[rows, :])
    rates = [jnp.exp(t) for t in last]
    state = ends[0]
    for k in range(1, STRETCHES):
        state = per_head(rates[k], state) + ends[k]
    pay[:, 0:ROWS, :] = state.astype(BF16).reshape(NS, ROWS, NST)
    grad = starts[STRETCHES - 1]
    for k in range(STRETCHES - 2, -1, -1):
        grad = per_head(rates[k], grad) + starts[k]
    pay[:, ROWS : 2 * ROWS, :] = grad.astype(BF16).reshape(NS, ROWS, NST)
    whole = functools.reduce(jnp.add, last)
    high = whole.astype(BF16).astype(F32)
    low = whole - high
    line = lax.broadcasted_iota(jnp.int32, (16, NST), 0)
    for r in range(NS):
        h = r // 2
        a = jnp.broadcast_to(high[0:1, h : h + 1], (16, NST))
        b = jnp.broadcast_to(low[0:1, h : h + 1], (16, NST))
        pay[r, 2 * ROWS : PAY, :] = jnp.where(
            line == 0, a, jnp.where(line == 1, b, 0.0)
        ).astype(BF16)


def scan_ends(x, g, ld, b, c):
    vm = pltpu.VMEM
    return call(
        ends_body,
        "scan_ends",
        [
            ((STRETCHES, WIDTH, NST), F32, vm),
            ((STRETCHES, WIDTH, NST), F32, vm),
            ((NS, PAY, NST), BF16, vm),
        ],
        [vm] * 5,
        [],
        2 * 2 * TOK * WIDTH * NST * 4,
        8 << 20,
    )(x, g, ld, b, c)


def prefix_body(inp, out):
    def forward(j, state):
        out[j, 0:ROWS, :] = state.astype(BF16)
        rest = inp[j, 2 * ROWS : PAY, :].astype(F32)
        rate = jnp.exp(rest[0:1, :] + rest[1:2, :])
        return rate * state + inp[j, 0:ROWS, :].astype(F32)

    def backward(t, grad):
        j = NS - 1 - t
        out[j, ROWS : 2 * ROWS, :] = grad.astype(BF16)
        rest = inp[j, 2 * ROWS : PAY, :].astype(F32)
        rate = jnp.exp(rest[0:1, :] + rest[1:2, :])
        return rate * grad + inp[j, ROWS : 2 * ROWS, :].astype(F32)

    zero = jnp.zeros((ROWS, NST), F32)
    lax.fori_loop(0, NS, forward, zero)
    lax.fori_loop(0, NS, backward, zero)


def scan_prefix(inp):
    vm = pltpu.VMEM
    return call(
        prefix_body,
        "scan_prefix",
        [((NS, 2 * ROWS, NST), BF16, vm)],
        [vm],
        [],
        0,
        2 << 20,
    )(inp)[0]


def grads_body(
    x_ref, g_ref, ld_ref, b_ref, c_ref, ends, starts, carried, dx_ref, dl_ref, bc_ref,
    states, grads, y_keep, d_keep,
):
    lower_mask = triangle(True)
    lower = lower_mask.astype(F32)
    upper = triangle(False).astype(F32)
    spread = head_map(False)
    gathered = head_map(True)
    ones = jnp.ones((8, NST), F32)
    rates = []
    for k in range(STRETCHES):
        ld = ld_ref[pl.ds(k * STRETCH, STRETCH), :]
        rates.append(jnp.exp(jnp.sum(ld, axis=0, keepdims=True)))
    state = carried[:, 0:ROWS, :].reshape(WIDTH, NST).astype(F32)
    states[0] = state.astype(BF16)
    for k in range(STRETCHES):
        state = per_head(rates[k], state) + ends[k]
        states[k + 1] = state.astype(BF16)
    grad = carried[:, ROWS : 2 * ROWS, :].reshape(WIDTH, NST).astype(F32)
    grads[STRETCHES - 1] = grad.astype(BF16)
    for k in range(STRETCHES - 1, 0, -1):
        grad = per_head(rates[k], grad) + starts[k]
        grads[k - 1] = grad.astype(BF16)

    def stretch(k, _):
        rows = pl.ds(pl.multiple_of(k * STRETCH, STRETCH), STRETCH)
        ld = ld_ref[rows, :]
        cumul = dot(lower, ld, ((1,), (0,)), HIGH)
        cumul_t = dot(ld, upper, ((0,), (0,)), HIGH)
        tot = cumul[STRETCH - 1 : STRETCH, :]
        b = b_ref[rows, :]
        c = c_ref[rows, :]
        cb = jnp.where(lower_mask, mm_nt(c, b), 0.0)
        mixed = jnp.zeros((STRETCH, STRETCH), F32)
        for h in range(SH):
            cols = pl.ds(h * HP, HP)
            x_h = x_ref[rows, cols]
            g_h = g_ref[rows, cols]
            gap = jnp.minimum(cumul[:, h : h + 1] - cumul_t[h : h + 1, :], 0.0)
            decay = jnp.exp(gap)
            weight = (decay * cb).astype(BF16)
            mixed = mixed + decay * mm_nt(g_h, x_h)
            y_keep[:, cols] = mm(weight, x_h)
            d_keep[:, cols] = mm_tn(weight, g_h)
        mixed = jnp.where(lower_mask, mixed, 0.0).astype(BF16)
        state = states[k]
        grad = grads[k]
        lead = two_part(jnp.exp(cumul), spread)
        tail = two_part(jnp.exp(tot - cumul), spread)
        x = x_ref[rows, :].astype(F32)
        g = g_ref[rows, :].astype(F32)
        y = y_keep[...] + lead * mm_nt(c, state)
        d = d_keep[...] + tail * mm_nt(b, grad)
        dx_ref[rows, :] = d.astype(BF16)
        bc_ref[rows, :] = (mm_tn(mixed, c) + mm((tail * x).astype(BF16), grad)).astype(BF16)
        c_rows = pl.ds(pl.multiple_of(TOK + k * STRETCH, STRETCH), STRETCH)
        bc_ref[c_rows, :] = (mm(mixed, b) + mm((lead * g).astype(BF16), state)).astype(BF16)
        change = two_part(g * y - x * d, gathered)
        meet = grad.astype(F32) * states[k + 1].astype(F32)
        meet = jnp.sum(meet.reshape(SH, HP, NST), axis=1)
        edge = dot(ones, meet, ((1,), (1,)), HIGH)[0:1, :]
        dl_ref[rows, :] = dot(upper, change, ((1,), (0,)), HIGH) + edge
        return 0

    lax.fori_loop(0, STRETCHES, stretch, 0)


def scan_grads(x, g, ld, b, c, ends, starts, carried):
    vm = pltpu.VMEM
    return call(
        grads_body,
        "scan_grads",
        [
            ((TOK, WIDTH), BF16, vm),
            ((TOK, SH), F32, vm),
            ((2 * TOK, NST), BF16, vm),
        ],
        [vm] * 8,
        [
            vm((STRETCHES + 1, WIDTH, NST), BF16),
            vm((STRETCHES, WIDTH, NST), BF16),
            vm((STRETCH, WIDTH), F32),
            vm((STRETCH, WIDTH), F32),
        ],
        2 * 8 * TOK * WIDTH * NST * 4,
        12 << 20,
    )(x, g, ld, b, c, ends, starts, carried)


def exchange(value, groups=None):
    return lax.all_to_all(value, "seq", 0, 0, tiled=True, axis_index_groups=groups)


def run(cap, codes, me, q, k, v, o, x, ld, b, c, g):
    heads = range(q.shape[1])
    columns = []
    for h in heads:
        kv = jnp.stack([k[:, h], v[:, h]])
        columns.append(lax.all_gather(kv, "seq", axis_index_groups=Z_GROUPS))
    ends, starts, pay = scan_ends(x, g, ld, b, c)
    carried = exchange(scan_prefix(exchange(pay)))
    dqs, dks, dvs = [], [], []
    for h in heads:
        incoming = exchange(gather_blocks(cap, codes, me, columns[h]), X_GROUPS)
        dq, near, far = attend(cap, codes, me, q[:, h], k[:, h], v[:, h], o[:, h], incoming)
        back = exchange(far.reshape(NX, cap, 2, BLK, HD), X_GROUPS)
        summed = lax.psum_scatter(
            combine(codes, me, back), "seq", scatter_dimension=0, axis_index_groups=Z_GROUPS
        )
        kv_grad = (near + summed.astype(F32)).astype(BF16)
        dqs.append(dq)
        dks.append(kv_grad[0])
        dvs.append(kv_grad[1])
    dx, dl, bc = scan_grads(x, g, ld, b, c, ends, starts, carried)
    shares = lax.all_to_all(bc.reshape(8, 128, NST), "head", 0, 0, tiled=True)
    part = jnp.sum(shares.astype(F32), axis=0).astype(BF16)
    whole = lax.all_gather(part, "head", tiled=True).astype(F32)
    return (
        jnp.stack(dqs, axis=1),
        jnp.stack(dks, axis=1),
        jnp.stack(dvs, axis=1),
        dx,
        dl,
        whole[:TOK],
        whole[TOK:],
    )


def per_device(q, k, v, o, x, ld, b, c, g, owner, offset, count):
    me = lax.axis_index("seq").astype(jnp.int32).reshape(1)
    live = jnp.arange(GLOB)[None, :] < count[:, None]
    codes = jnp.where(live, owner * SEG + offset, -1).reshape(NS * ITEMS)
    column = jnp.where(live, owner >> 3, -1).reshape(NS, ITEMS)
    named = jnp.sum(
        (column[:, :, None] == jnp.arange(NX)[None, None, :]).astype(jnp.int32), axis=1
    )
    args = (codes, me, q, k, v, o, x, ld, b, c, g)
    return lax.cond(
        jnp.max(named) <= FAST,
        functools.partial(run, FAST),
        functools.partial(run, ITEMS),
        *args,
    )


def solution(mesh):
    wide = P("seq", "head", None)
    flat = P("seq", "head")
    own = P("seq", None)
    return jax.shard_map(
        per_device,
        mesh=mesh,
        in_specs=(wide, wide, wide, wide, flat, flat, own, own, flat, P(), P(), P()),
        out_specs=(wide, wide, wide, flat, flat, own, own),
        check_vma=False,
    )
```

```python
import functools
import math

import jax
import jax.numpy as jnp
from jax import lax
from jax.experimental import pallas as pl
from jax.experimental.pallas import tpu as pltpu
from jax.sharding import PartitionSpec as P

HD = 128
HP = 64
NST = 128
BLK = 128
STRETCH = 128
SEG = 4
GLOB = 4
TOK = 512
SH = 16
WIDTH = SH * HP
ITEMS = SEG * GLOB
NX = 4
NZ = 8
NS = NX * NZ
ROWS = WIDTH // NS
PAY = 2 * ROWS + 16
STRETCHES = TOK // STRETCH

HIGH = lax.Precision.HIGHEST
F32 = jnp.float32
BF16 = jnp.bfloat16
Z_GROUPS = [[x * NZ + z for z in range(NZ)] for x in range(NX)]
X_GROUPS = [[x * NZ + z for x in range(NX)] for z in range(NZ)]


def dot(a, b, dims, precision=None):
    return lax.dot_general(
        a, b, (dims, ((), ())), precision=precision, preferred_element_type=F32
    )


def mm(a, b):
    return dot(a, b, ((1,), (0,)))


def mm_nt(a, b):
    return dot(a, b, ((1,), (1,)))


def mm_tn(a, b):
    return dot(a, b, ((0,), (0,)))


def call(body, name, outs, ins, scratch, flops, nbytes, vmem=48 << 20):
    return pl.pallas_call(
        body,
        out_shape=[jax.ShapeDtypeStruct(s, d) for s, d, _ in outs],
        in_specs=[pl.BlockSpec(memory_space=m) for m in ins],
        out_specs=[pl.BlockSpec(memory_space=m) for _, _, m in outs],
        scratch_shapes=scratch,
        compiler_params=pltpu.CompilerParams(vmem_limit_bytes=vmem),
        cost_estimate=pl.CostEstimate(flops=flops, bytes_accessed=nbytes, transcendentals=0),
        name=name,
    )


SCALE = 1.0 / math.sqrt(HD)
EMPTY = -1e30
KINDS = 3
FAR = NZ * SEG


def list_items(codes, me, places, blocks):
    here = me[0]
    my_x = here >> 3
    my_z = here & (NZ - 1)
    count = jnp.int32(0)
    for d in range(NX):
        base = (((my_x - d) & (NX - 1)) * NZ + my_z) * ITEMS

        def item(i, n, d=d, base=base):
            code = codes[base + i]
            places[n] = code & (FAR - 1)
            blocks[n] = d * SEG + (i >> 2)
            return n + ((code >= 0) & ((code >> 5) == my_x)).astype(jnp.int32)

        count = lax.fori_loop(0, ITEMS, item, count)
    places[count] = 0
    blocks[count] = NX * SEG
    return count


def span(index):
    return pl.ds(pl.multiple_of(index * BLK, BLK), BLK)


def pairs(count, visit):
    def two(t, _):
        visit([2 * t, 2 * t + 1])
        return 0

    lax.fori_loop(0, (count + 1) >> 1, two, 0)


def fetch(qos, keys, place, block):
    d = jnp.minimum(block >> 2, NX - 1)
    rows = span(block & (SEG - 1))
    z = place >> 2
    cols = span(place & (SEG - 1))
    return [
        (qos[d, h, 0, rows, :], qos[d, h, 1, rows, :], keys[z, h, 0, cols, :], keys[z, h, 1, cols, :])
        for h in range(2)
    ]


def summary(q, o, k, v):
    s = mm_nt(k, q) * SCALE
    dp = mm_nt(v, o)
    m = jnp.max(s, axis=0, keepdims=True)
    e = jnp.exp(s - m)
    return m, jnp.sum(e, axis=0, keepdims=True), jnp.sum(e * dp, axis=0, keepdims=True)


def stack_rows(rows):
    return jnp.concatenate(rows + [jnp.zeros((8 - len(rows), rows[0].shape[1]), F32)], axis=0)


def near_stats_body(qo, kv, out):
    for b in range(SEG):
        rows = pl.ds(b * BLK, BLK)
        parts = []
        for h in range(2):
            parts += summary(qo[h, 0, rows, :], qo[h, 1, rows, :], kv[h, 0], kv[h, 1])
        out[:, rows] = stack_rows(parts)


def near_stats(qo, kv):
    vm = pltpu.VMEM
    return call(
        near_stats_body,
        "near_stats",
        [((8, TOK), F32, vm)],
        [vm, vm],
        [],
        2 * 2 * 2 * TOK * TOK * HD,
        1 << 20,
    )(qo, kv)[0]


def far_stats_body(codes, me, near, column, qos, out, tally, places, blocks):
    count = list_items(codes, me, places, blocks)
    kind = lax.broadcasted_iota(jnp.int32, (8, BLK), 0)
    start = jnp.where((kind == 0) | (kind == KINDS), EMPTY, 0.0)
    for n in range(NX * SEG + 1):
        tally[n] = start

    def visit(items):
        found = []
        for n in items:
            found.append([summary(*part) for part in fetch(qos, column, places[n], blocks[n])])
        for n, heads in zip(items, found):
            old = tally[blocks[n]]
            rows = []
            for h, (m, l, t) in enumerate(heads):
                m0, l0, t0 = [old[KINDS * h + i : KINDS * h + i + 1, :] for i in range(KINDS)]
                high = jnp.maximum(m0, m)
                f0 = jnp.exp(m0 - high)
                f1 = jnp.exp(m - high)
                rows += [high, l0 * f0 + l * f1, t0 * f0 + t * f1]
            tally[blocks[n]] = stack_rows(rows)

    pairs(count, visit)
    for d in range(NX):
        for b in range(SEG):
            out[d, :, pl.ds(b * BLK, BLK)] = tally[d * SEG + b]
    out[NX] = near[...]


def item_scratch():
    return [pltpu.SMEM((NX * ITEMS + 1,), jnp.int32)] * 2


def far_stats(codes, me, near, column, qos):
    vm = pltpu.VMEM
    return call(
        far_stats_body,
        "far_stats",
        [((NX + 1, 8, TOK), F32, vm)],
        [pltpu.SMEM, pltpu.SMEM] + [vm] * 3,
        [vm((NX * SEG + 1, 8, BLK), F32)] + item_scratch(),
        2 * 2 * 2 * 16 * BLK * BLK * HD,
        6 << 20,
    )(codes, me, near, column, qos)[0]


def joined(stats, my_x, x_q):
    parts = []
    for r in range(NX):
        x = (my_x - r) & (NX - 1)
        parts.append(stats[r, (x - x_q) & (NX - 1)])
    parts.append(stats[(my_x - x_q) & (NX - 1), NX])
    rows = []
    for h in range(2):
        at = KINDS * h
        high = functools.reduce(jnp.maximum, [p[at : at + 1, :] for p in parts])
        fade = [jnp.exp(p[at : at + 1, :] - high) for p in parts]
        total = sum(f * p[at + 1 : at + 2, :] for f, p in zip(fade, parts))
        mixed = sum(f * p[at + 2 : at + 3, :] for f, p in zip(fade, parts))
        inverse = 1.0 / total
        rows += [high, inverse, mixed * inverse]
    return stack_rows(rows)


def weights_of(q, o, k, v, row):
    high, inverse, delta = [row[i : i + 1, :] for i in range(KINDS)]
    p = jnp.exp(mm_nt(k, q) * SCALE - high) * inverse
    ds = (p * (mm_nt(v, o) - delta) * SCALE).astype(BF16)
    return p.astype(BF16), ds


def far_grads_body(
    codes, me, stats, column, qos, kv_out, dq_out, total, dq, rowed, places, blocks
):
    my_x = me[0] >> 3
    count = list_items(codes, me, places, blocks)
    total[...] = jnp.zeros_like(total)
    dq[...] = jnp.zeros_like(dq)
    for d in range(NX):
        row = joined(stats, my_x, (my_x - d) & (NX - 1))
        for b in range(SEG):
            rowed[d * SEG + b] = row[:, b * BLK : (b + 1) * BLK]
    rowed[NX * SEG] = jnp.zeros((8, BLK), F32)

    def visit(items):
        found = []
        for n in items:
            row = rowed[blocks[n]]
            heads = fetch(qos, column, places[n], blocks[n])
            grads = []
            for h, (q, o, k, v) in enumerate(heads):
                p, ds = weights_of(q, o, k, v, row[KINDS * h : KINDS * h + KINDS, :])
                grads.append((mm_tn(ds, k), mm(ds, q), mm(p, o)))
            found.append(grads)
        for n, grads in zip(items, found):
            at = blocks[n]
            to = jnp.where(at == NX * SEG, FAR, places[n])
            for h, (dqh, dkh, dvh) in enumerate(grads):
                dq[at, h] += dqh
                total[to, h, 0] += dkh
                total[to, h, 1] += dvh

    pairs(count, visit)
    for d in range(NX):
        for b in range(SEG):
            dq_out[(my_x - d) & (NX - 1), :, pl.ds(b * BLK, BLK), :] = dq[d * SEG + b].astype(BF16)
    for z in range(NZ):
        for h in range(2):
            for s in range(2):
                for b in range(SEG):
                    at = (2 * h + s) * TOK + b * BLK
                    kv_out[z, pl.ds(at, BLK), :] = total[z * SEG + b, h, s].astype(BF16)


def far_grads(codes, me, stats, column, qos):
    vm = pltpu.VMEM
    return call(
        far_grads_body,
        "far_grads",
        [((NZ, 4 * TOK, HD), BF16, vm), ((NX, 2, TOK, HD), BF16, vm)],
        [pltpu.SMEM, pltpu.SMEM] + [vm] * 3,
        [
            vm((FAR + 1, 2, 2, BLK, HD), F32),
            vm((NX * SEG + 1, 2, BLK, HD), F32),
            vm((NX * SEG + 1, 8, BLK), F32),
        ]
        + item_scratch(),
        5 * 2 * 2 * 16 * BLK * BLK * HD,
        12 << 20,
    )(codes, me, stats, column, qos)


def near_grads_body(me, stats, qo, kv, dq_out, kv_out, p_keep, s_keep):
    my_x = me[0] >> 3
    row = joined(stats, my_x, my_x)
    for h in range(2):
        k = kv[h, 0]
        for b in range(SEG):
            rows = pl.ds(b * BLK, BLK)
            p, ds = weights_of(
                qo[h, 0, rows, :], qo[h, 1, rows, :], k, kv[h, 1],
                row[KINDS * h : KINDS * h + KINDS, b * BLK : (b + 1) * BLK],
            )
            dq_out[h, rows, :] = mm_tn(ds, k)
            p_keep[:, rows] = p
            s_keep[:, rows] = ds
        kv_out[h, 0] = mm(s_keep[...], qo[h, 0])
        kv_out[h, 1] = mm(p_keep[...], qo[h, 1])


def near_grads(me, stats, qo, kv):
    vm = pltpu.VMEM
    return call(
        near_grads_body,
        "near_grads",
        [((2, TOK, HD), F32, vm), ((2, 2, TOK, HD), F32, vm)],
        [pltpu.SMEM] + [vm] * 3,
        [vm((TOK, TOK), BF16), vm((TOK, TOK), BF16)],
        5 * 2 * 2 * TOK * TOK * HD,
        4 << 20,
    )(me, stats, qo, kv)


def triangle(lower):
    i = lax.broadcasted_iota(jnp.int32, (STRETCH, STRETCH), 0)
    j = lax.broadcasted_iota(jnp.int32, (STRETCH, STRETCH), 1)
    return i >= j if lower else i <= j


def head_map(transposed):
    shape = (WIDTH, SH) if transposed else (SH, WIDTH)
    wide = lax.broadcasted_iota(jnp.int32, shape, 0 if transposed else 1)
    head = lax.broadcasted_iota(jnp.int32, shape, 1 if transposed else 0)
    return ((wide >> 6) == head).astype(BF16)


def two_part(a, b):
    high = a.astype(BF16)
    low = (a - high.astype(F32)).astype(BF16)
    return mm(high, b) + mm(low, b)


def per_head(rates, state):
    return jnp.concatenate(
        [state[h * HP : (h + 1) * HP, :] * rates[0:1, h : h + 1] for h in range(SH)], axis=0
    )


def ends_body(x_ref, g_ref, ld_ref, b_ref, c_ref, ends, starts, pay):
    lower = triangle(True).astype(F32)
    spread = head_map(False)
    last = []
    for k in range(STRETCHES):
        rows = pl.ds(k * STRETCH, STRETCH)
        cumul = dot(lower, ld_ref[rows, :], ((1,), (0,)), HIGH)
        tot = cumul[STRETCH - 1 : STRETCH, :]
        last.append(tot)
        tail = two_part(jnp.exp(tot - cumul), spread)
        lead = two_part(jnp.exp(cumul), spread)
        x_in = (x_ref[rows, :].astype(F32) * tail).astype(BF16)
        g_in = (g_ref[rows, :].astype(F32) * lead).astype(BF16)
        ends[k] = mm_tn(x_in, b_ref[rows, :])
        starts[k] = mm_tn(g_in, c_ref[rows, :])
    rates = [jnp.exp(t) for t in last]
    state = ends[0]
    for k in range(1, STRETCHES):
        state = per_head(rates[k], state) + ends[k]
    pay[:, 0:ROWS, :] = state.astype(BF16).reshape(NS, ROWS, NST)
    grad = starts[STRETCHES - 1]
    for k in range(STRETCHES - 2, -1, -1):
        grad = per_head(rates[k], grad) + starts[k]
    pay[:, ROWS : 2 * ROWS, :] = grad.astype(BF16).reshape(NS, ROWS, NST)
    whole = functools.reduce(jnp.add, last)
    high = whole.astype(BF16).astype(F32)
    low = whole - high
    line = lax.broadcasted_iota(jnp.int32, (16, NST), 0)
    for r in range(NS):
        h = r // 2
        a = jnp.broadcast_to(high[0:1, h : h + 1], (16, NST))
        b = jnp.broadcast_to(low[0:1, h : h + 1], (16, NST))
        pay[r, 2 * ROWS : PAY, :] = jnp.where(
            line == 0, a, jnp.where(line == 1, b, 0.0)
        ).astype(BF16)


def scan_ends(x, g, ld, b, c):
    vm = pltpu.VMEM
    return call(
        ends_body,
        "scan_ends",
        [
            ((STRETCHES, WIDTH, NST), F32, vm),
            ((STRETCHES, WIDTH, NST), F32, vm),
            ((NS, PAY, NST), BF16, vm),
        ],
        [vm] * 5,
        [],
        2 * 2 * TOK * WIDTH * NST * 4,
        8 << 20,
    )(x, g, ld, b, c)


def prefix_body(inp, out):
    def forward(j, state):
        out[j, 0:ROWS, :] = state.astype(BF16)
        rest = inp[j, 2 * ROWS : PAY, :].astype(F32)
        rate = jnp.exp(rest[0:1, :] + rest[1:2, :])
        return rate * state + inp[j, 0:ROWS, :].astype(F32)

    def backward(t, grad):
        j = NS - 1 - t
        out[j, ROWS : 2 * ROWS, :] = grad.astype(BF16)
        rest = inp[j, 2 * ROWS : PAY, :].astype(F32)
        rate = jnp.exp(rest[0:1, :] + rest[1:2, :])
        return rate * grad + inp[j, ROWS : 2 * ROWS, :].astype(F32)

    zero = jnp.zeros((ROWS, NST), F32)
    lax.fori_loop(0, NS, forward, zero)
    lax.fori_loop(0, NS, backward, zero)


def scan_prefix(inp):
    vm = pltpu.VMEM
    return call(
        prefix_body,
        "scan_prefix",
        [((NS, 2 * ROWS, NST), BF16, vm)],
        [vm],
        [],
        0,
        2 << 20,
    )(inp)[0]


def grads_body(
    x_ref, g_ref, ld_ref, b_ref, c_ref, ends, starts, carried, dx_ref, dl_ref, bc_ref,
    states, grads, y_keep, d_keep,
):
    lower_mask = triangle(True)
    lower = lower_mask.astype(F32)
    upper = triangle(False).astype(F32)
    spread = head_map(False)
    gathered = head_map(True)
    ones = jnp.ones((8, NST), F32)
    rates = []
    for k in range(STRETCHES):
        ld = ld_ref[pl.ds(k * STRETCH, STRETCH), :]
        rates.append(jnp.exp(jnp.sum(ld, axis=0, keepdims=True)))
    state = carried[:, 0:ROWS, :].reshape(WIDTH, NST).astype(F32)
    states[0] = state.astype(BF16)
    for k in range(STRETCHES):
        state = per_head(rates[k], state) + ends[k]
        states[k + 1] = state.astype(BF16)
    grad = carried[:, ROWS : 2 * ROWS, :].reshape(WIDTH, NST).astype(F32)
    grads[STRETCHES - 1] = grad.astype(BF16)
    for k in range(STRETCHES - 1, 0, -1):
        grad = per_head(rates[k], grad) + starts[k]
        grads[k - 1] = grad.astype(BF16)

    def stretch(k, _):
        rows = pl.ds(pl.multiple_of(k * STRETCH, STRETCH), STRETCH)
        ld = ld_ref[rows, :]
        cumul = dot(lower, ld, ((1,), (0,)), HIGH)
        cumul_t = dot(ld, upper, ((0,), (0,)), HIGH)
        tot = cumul[STRETCH - 1 : STRETCH, :]
        b = b_ref[rows, :]
        c = c_ref[rows, :]
        cb = jnp.where(lower_mask, mm_nt(c, b), 0.0)
        mixed = jnp.zeros((STRETCH, STRETCH), F32)
        for h in range(SH):
            cols = pl.ds(h * HP, HP)
            x_h = x_ref[rows, cols]
            g_h = g_ref[rows, cols]
            gap = jnp.minimum(cumul[:, h : h + 1] - cumul_t[h : h + 1, :], 0.0)
            decay = jnp.exp(gap)
            weight = (decay * cb).astype(BF16)
            mixed = mixed + decay * mm_nt(g_h, x_h)
            y_keep[:, cols] = mm(weight, x_h)
            d_keep[:, cols] = mm_tn(weight, g_h)
        mixed = jnp.where(lower_mask, mixed, 0.0).astype(BF16)
        state = states[k]
        grad = grads[k]
        lead = two_part(jnp.exp(cumul), spread)
        tail = two_part(jnp.exp(tot - cumul), spread)
        x = x_ref[rows, :].astype(F32)
        g = g_ref[rows, :].astype(F32)
        y = y_keep[...] + lead * mm_nt(c, state)
        d = d_keep[...] + tail * mm_nt(b, grad)
        dx_ref[rows, :] = d.astype(BF16)
        bc_ref[rows, :] = (mm_tn(mixed, c) + mm((tail * x).astype(BF16), grad)).astype(BF16)
        c_rows = pl.ds(pl.multiple_of(TOK + k * STRETCH, STRETCH), STRETCH)
        bc_ref[c_rows, :] = (mm(mixed, b) + mm((lead * g).astype(BF16), state)).astype(BF16)
        change = two_part(g * y - x * d, gathered)
        meet = grad.astype(F32) * states[k + 1].astype(F32)
        meet = jnp.sum(meet.reshape(SH, HP, NST), axis=1)
        edge = dot(ones, meet, ((1,), (1,)), HIGH)[0:1, :]
        dl_ref[rows, :] = dot(upper, change, ((1,), (0,)), HIGH) + edge
        return 0

    lax.fori_loop(0, STRETCHES, stretch, 0)


def scan_grads(x, g, ld, b, c, ends, starts, carried):
    vm = pltpu.VMEM
    return call(
        grads_body,
        "scan_grads",
        [
            ((TOK, WIDTH), BF16, vm),
            ((TOK, SH), F32, vm),
            ((2 * TOK, NST), BF16, vm),
        ],
        [vm] * 8,
        [
            vm((STRETCHES + 1, WIDTH, NST), BF16),
            vm((STRETCHES, WIDTH, NST), BF16),
            vm((STRETCH, WIDTH), F32),
            vm((STRETCH, WIDTH), F32),
        ],
        2 * 8 * TOK * WIDTH * NST * 4,
        12 << 20,
    )(x, g, ld, b, c, ends, starts, carried)


def exchange(value, groups=None):
    return lax.all_to_all(value, "seq", 0, 0, tiled=True, axis_index_groups=groups)


def along_x(value, step):
    pairs = [
        (x * NZ + z, (x + step) % NX * NZ + z) for x in range(NX) for z in range(NZ)
    ]
    return lax.ppermute(value, "seq", pairs)


def after(value, *earlier):
    return lax.optimization_barrier((value, earlier))[0]


def per_device(q, k, v, o, x, ld, b, c, g, owner, offset, count):
    me = lax.axis_index("seq").astype(jnp.int32).reshape(1)
    live = jnp.arange(GLOB)[None, :] < count[:, None]
    codes = jnp.where(live, owner * SEG + offset, -1).reshape(NS * ITEMS)
    heads = range(q.shape[1])
    kv = jnp.stack([jnp.stack([k[:, h], v[:, h]]) for h in heads])
    qo = jnp.stack([jnp.stack([q[:, h], o[:, h]]) for h in heads])
    column = lax.all_gather(kv, "seq", axis_index_groups=Z_GROUPS)
    qos = jnp.stack([qo] + [along_x(qo, d) for d in range(1, NX)])
    near = near_stats(qo, kv)
    ends, starts, pay = scan_ends(x, g, ld, b, c)
    pay = exchange(after(pay, qos))
    carried = exchange(scan_prefix(after(pay, column)))
    column = after(column, pay)
    stats = far_stats(codes, me, near, column, qos)
    stats = jnp.stack([stats] + [along_x(stats, d) for d in range(1, NX)])
    stats = after(stats, carried)
    kv_far, dq_far = far_grads(codes, me, stats, column, qos)
    kv_far = lax.psum_scatter(
        kv_far, "seq", scatter_dimension=0, axis_index_groups=Z_GROUPS
    )
    carried = after(carried, dq_far)
    dq_far = exchange(dq_far, X_GROUPS)
    dx, dl, bc = scan_grads(x, g, ld, b, c, ends, starts, carried)
    shares = lax.all_to_all(bc.reshape(8, 128, NST), "head", 0, 0, tiled=True)
    part = jnp.sum(shares.astype(F32), axis=0).astype(BF16)
    whole = lax.all_gather(part, "head", tiled=True).astype(F32)
    dq_near, kv_near = near_grads(me, after(stats, dq_far), qo, kv)
    dq = (dq_near + jnp.sum(dq_far.astype(F32), axis=0)).astype(BF16)
    kv_grad = (kv_near + kv_far.astype(F32).reshape(kv_near.shape)).astype(BF16)
    return (
        jnp.swapaxes(dq, 0, 1),
        jnp.swapaxes(kv_grad[:, 0], 0, 1),
        jnp.swapaxes(kv_grad[:, 1], 0, 1),
        dx,
        dl,
        whole[:TOK],
        whole[TOK:],
    )


def solution(mesh):
    wide = P("seq", "head", None)
    flat = P("seq", "head")
    own = P("seq", None)
    return jax.shard_map(
        per_device,
        mesh=mesh,
        in_specs=(wide, wide, wide, wide, flat, flat, own, own, flat, P(), P(), P()),
        out_specs=(wide, wide, wide, flat, flat, own, own),
        check_vma=False,
    )
```

```python
import functools
import math

import jax
import jax.numpy as jnp
from jax import lax
from jax.experimental import pallas as pl
from jax.experimental.pallas import tpu as pltpu
from jax.sharding import PartitionSpec as P

HD = 128
HP = 64
NST = 128
BLK = 128
STRETCH = 128
SEG = 4
GLOB = 4
TOK = 512
SH = 16
WIDTH = SH * HP
ITEMS = SEG * GLOB
NX = 4
NZ = 8
NS = NX * NZ
ROWS = WIDTH // NS
PAY = 2 * ROWS + 16
STRETCHES = TOK // STRETCH

HIGH = lax.Precision.HIGHEST
F32 = jnp.float32
BF16 = jnp.bfloat16
Z_GROUPS = [[x * NZ + z for z in range(NZ)] for x in range(NX)]
X_GROUPS = [[x * NZ + z for x in range(NX)] for z in range(NZ)]


def dot(a, b, dims, precision=None):
    return lax.dot_general(
        a, b, (dims, ((), ())), precision=precision, preferred_element_type=F32
    )


def mm(a, b):
    return dot(a, b, ((1,), (0,)))


def mm_nt(a, b):
    return dot(a, b, ((1,), (1,)))


def mm_tn(a, b):
    return dot(a, b, ((0,), (0,)))


def call(body, name, outs, ins, scratch, flops, nbytes, vmem=48 << 20):
    return pl.pallas_call(
        body,
        out_shape=[jax.ShapeDtypeStruct(s, d) for s, d, _ in outs],
        in_specs=[pl.BlockSpec(memory_space=m) for m in ins],
        out_specs=[pl.BlockSpec(memory_space=m) for _, _, m in outs],
        scratch_shapes=scratch,
        compiler_params=pltpu.CompilerParams(vmem_limit_bytes=vmem),
        cost_estimate=pl.CostEstimate(flops=flops, bytes_accessed=nbytes, transcendentals=0),
        name=name,
    )


SCALE = 1.0 / math.sqrt(HD)
EMPTY = -1e30
KINDS = 3
FAR = NZ * SEG
UNROLL = 4
PAIR = 2 * HD


def far_items(codes, me):
    my_x = me[0] >> 3
    my_z = me[0] & (NZ - 1)
    sources = ((my_x - jnp.arange(NX)) & (NX - 1)) * NZ + my_z
    code = jnp.take(codes.reshape(NS, ITEMS), sources, axis=0).reshape(NX * ITEMS)
    block = jnp.arange(NX * ITEMS) // GLOB
    hit = (code >= 0) & ((code >> 5) == my_x)
    order = jnp.arange(NX * ITEMS)
    rank = jnp.sum((hit[None, :] & (order[None, :] < order[:, None])).astype(jnp.int32), axis=1)
    slot = jnp.arange(NX * ITEMS + UNROLL)[:, None]
    chosen = hit[None, :] & (rank[None, :] == slot)
    places = jnp.sum(jnp.where(chosen, code[None, :] & (FAR - 1), 0), axis=1)
    blocks = NX * SEG + jnp.sum(jnp.where(chosen, block[None, :] - NX * SEG, 0), axis=1)
    count = jnp.sum(hit.astype(jnp.int32)).reshape(1)
    return jnp.concatenate([count, places, blocks]).astype(jnp.int32)


class Listed:
    def __init__(self, ref):
        self.count = ref[0]
        self.place = lambda n: ref[1 + n]
        self.block = lambda n: ref[1 + NX * ITEMS + UNROLL + n]


def span(index):
    return pl.ds(pl.multiple_of(index * BLK, BLK), BLK)


def in_groups(count, visit):
    def group(t, _):
        visit([UNROLL * t + i for i in range(UNROLL)])
        return 0

    lax.fori_loop(0, (count + UNROLL - 1) // UNROLL, group, 0)


def head(h):
    return pl.ds(h * HD, HD)


def summary(q, o, k, v):
    s = mm_nt(k, q) * SCALE
    dp = mm_nt(v, o)
    m = jnp.max(s, axis=0, keepdims=True)
    e = jnp.exp(s - m)
    return [m, jnp.sum(e, axis=0, keepdims=True), jnp.sum(e * dp, axis=0, keepdims=True)]


def packed(quads):
    return jnp.concatenate(
        [jnp.concatenate([quads[i], quads[i + 2]], axis=0) for i in range(2)], axis=1
    )


def unpacked(tile, b):
    at = 4 * (b >> 1)
    return tile[at : at + KINDS, (b & 1) * PAIR : (b & 1) * PAIR + PAIR]


def near_stats_body(qo, kv, out):
    quads = []
    for b in range(SEG):
        rows = pl.ds(b * BLK, BLK)
        heads = [
            summary(qo[0, rows, head(h)], qo[1, rows, head(h)], kv[0, :, head(h)], kv[1, :, head(h)])
            for h in range(2)
        ]
        quads.append(
            jnp.concatenate(
                [jnp.concatenate([x, y], axis=1) for x, y in zip(*heads)]
                + [jnp.zeros((1, PAIR), F32)],
                axis=0,
            )
        )
    out[...] = packed(quads)


def near_stats(qo, kv):
    vm = pltpu.VMEM
    return call(
        near_stats_body,
        "near_stats",
        [((8, 2 * PAIR), F32, vm)],
        [vm, vm],
        [],
        2 * 2 * 2 * TOK * TOK * HD,
        1 << 20,
    )(qo, kv)[0]


def spread(value):
    lane = lax.broadcasted_iota(jnp.int32, (BLK, PAIR), 1)
    zero = jnp.zeros((BLK, PAIR), BF16)
    return jnp.concatenate(
        [jnp.where(lane < HD, value, zero), jnp.where(lane < HD, zero, value)], axis=0
    )


def load(pieces, sems):
    copies = [pltpu.make_async_copy(a, b, sems.at[i]) for i, (a, b) in enumerate(pieces)]
    for copy in copies:
        copy.start()

    def wait():
        for copy in copies:
            copy.wait()

    return wait


def load_far(column_in, qos_in, column, qos, sems):
    return load(
        [(column_in.at[z], column.at[z]) for z in range(NZ)]
        + [(qos_in.at[d], qos.at[d]) for d in range(NX)],
        sems,
    )


def far_scratch():
    return [
        pltpu.VMEM((NZ, 2, TOK, PAIR), BF16),
        pltpu.VMEM((NX, 2, TOK, PAIR), BF16),
        pltpu.SemaphoreType.DMA((NZ + NX,)),
    ]


def fetch(qos, keys, place, block):
    n = jnp.minimum(block, NX * SEG - 1)
    d = n >> 2
    rows = span(n & (SEG - 1))
    z = place >> 2
    cols = span(place & (SEG - 1))
    return (
        spread(qos[d, 0, rows, :]), spread(qos[d, 1, rows, :]), keys[z, 0, cols, :], keys[z, 1, cols, :]
    )


def far_stats_body(listed, near, column_in, qos_in, out, tally, column, qos, sems):
    ready = load_far(column_in, qos_in, column, qos, sems)
    items = Listed(listed)
    kind = lax.broadcasted_iota(jnp.int32, (4, PAIR), 0)
    start = jnp.where(kind == 0, EMPTY, 0.0)
    for n in range(NX * SEG + 1):
        tally[n] = start
    ready()

    def visit(numbers):
        found = [summary(*fetch(qos, column, items.place(n), items.block(n))) for n in numbers]
        for n, (m, l, t) in zip(numbers, found):
            old = tally[items.block(n)]
            m0, l0, t0 = [old[i : i + 1, :] for i in range(KINDS)]
            high = jnp.maximum(m0, m)
            f0 = jnp.exp(m0 - high)
            f1 = jnp.exp(m - high)
            tally[items.block(n)] = jnp.concatenate(
                [high, l0 * f0 + l * f1, t0 * f0 + t * f1, jnp.zeros_like(high)], axis=0
            )

    in_groups(items.count, visit)
    for d in range(NX):
        out[d] = packed([tally[d * SEG + b] for b in range(SEG)])
    out[NX] = near[...]


def far_stats(listed, near, column, qos):
    vm = pltpu.VMEM
    return call(
        far_stats_body,
        "far_stats",
        [((NX + 1, 8, 2 * PAIR), F32, vm)],
        [pltpu.SMEM, vm, pltpu.HBM, pl.ANY],
        [vm((NX * SEG + 1, 4, PAIR), F32)] + far_scratch(),
        2 * 2 * 2 * 16 * BLK * BLK * HD,
        6 << 20,
    )(listed, near, column, qos)[0]


def joined(stats, my_x, x_q):
    parts = []
    for r in range(NX):
        x = (my_x - r) & (NX - 1)
        parts.append(stats[r, (x - x_q) & (NX - 1)])
    parts.append(stats[(my_x - x_q) & (NX - 1), NX])
    rows = []
    for at in (0, 4):
        high = functools.reduce(jnp.maximum, [p[at : at + 1, :] for p in parts])
        fade = [jnp.exp(p[at : at + 1, :] - high) for p in parts]
        total = sum(f * p[at + 1 : at + 2, :] for f, p in zip(fade, parts))
        mixed = sum(f * p[at + 2 : at + 3, :] for f, p in zip(fade, parts))
        inverse = 1.0 / total
        rows += [high, inverse, mixed * inverse, jnp.zeros_like(high)]
    return jnp.concatenate(rows, axis=0)


def weights_of(q, o, k, v, row):
    high, inverse, delta = [row[i : i + 1, :] for i in range(KINDS)]
    p = jnp.exp(mm_nt(k, q) * SCALE - high) * inverse
    ds = (p * (mm_nt(v, o) - delta) * SCALE).astype(BF16)
    return p.astype(BF16), ds


def ds_copies(a, b, sems):
    def group(t):
        tiles = pl.ds(UNROLL * t, UNROLL)
        return pltpu.make_async_copy(a.at[tiles], b.at[tiles], sems.at[t])

    return group


def far_grads_body(
    listed, me, stats, column_in, qos_in, kv_out, ds_out,
    total, rowed, staged, ds_keep, column, qos, sems, out_sems, ds_sems,
):
    ready = load_far(column_in, qos_in, column, qos, sems)
    my_x = me[0] >> 3
    items = Listed(listed)
    sent = ds_copies(ds_keep, ds_out, ds_sems)
    total[...] = jnp.zeros_like(total)
    for d in range(NX):
        tile = joined(stats, my_x, (my_x - d) & (NX - 1))
        for b in range(SEG):
            rowed[d * SEG + b, 0:KINDS, :] = unpacked(tile, b)
    rowed[NX * SEG] = jnp.zeros((8, PAIR), F32)
    ready()

    def group(t, _):
        numbers = [UNROLL * t + i for i in range(UNROLL)]
        found = []
        for n in numbers:
            q, o, k, v = fetch(qos, column, items.place(n), items.block(n))
            p, ds = weights_of(q, o, k, v, rowed[items.block(n)])
            found.append((ds, mm(ds, q), mm(p, o)))
        for n, (ds, dk, dv) in zip(numbers, found):
            to = jnp.where(items.block(n) == NX * SEG, FAR, items.place(n))
            ds_keep[n] = ds
            total[to, 0] += dk
            total[to, 1] += dv
        sent(t).start()
        return 0

    groups = (items.count + UNROLL - 1) // UNROLL
    lax.fori_loop(0, groups, group, 0)
    copies = []
    for z in range(NZ):
        for s in range(2):
            for b in range(SEG):
                staged[z, pl.ds(s * TOK + b * BLK, BLK), :] = total[z * SEG + b, s].astype(BF16)
        copies.append(pltpu.make_async_copy(staged.at[z], kv_out.at[z], out_sems.at[z]))
        copies[-1].start()

    def drain(t, _):
        sent(t).wait()
        return 0

    lax.fori_loop(0, groups, drain, 0)
    for copy in copies:
        copy.wait()


def far_grads(listed, me, stats, column, qos):
    vm = pltpu.VMEM
    tiles = NX * ITEMS + UNROLL
    return call(
        far_grads_body,
        "far_grads",
        [
            ((NZ, 2 * TOK, PAIR), BF16, pltpu.HBM),
            ((tiles, BLK, PAIR), BF16, pltpu.HBM),
        ],
        [pltpu.SMEM, pltpu.SMEM, vm, pltpu.HBM, pl.ANY],
        [
            vm((FAR + 1, 2, BLK, PAIR), F32),
            vm((NX * SEG + 1, 8, PAIR), F32),
            vm((NZ, 2 * TOK, PAIR), BF16),
            vm((tiles, BLK, PAIR), BF16),
        ]
        + far_scratch()
        + [pltpu.SemaphoreType.DMA((NZ,)), pltpu.SemaphoreType.DMA((tiles // UNROLL,))],
        4 * 2 * 2 * 16 * BLK * BLK * HD,
        12 << 20,
    )(listed, me, stats, column, qos)


def far_queries_body(listed, me, ds_in, column_in, dq_out, dq, ds_keep, keys, sems, ds_sems):
    ready = load([(column_in.at[z, 0], keys.at[z]) for z in range(NZ)], sems)
    my_x = me[0] >> 3
    items = Listed(listed)
    fetched = ds_copies(ds_in, ds_keep, ds_sems)
    groups = (items.count + UNROLL - 1) // UNROLL

    def begin(t, _):
        fetched(t).start()
        return 0

    lax.fori_loop(0, groups, begin, 0)
    dq[...] = jnp.zeros_like(dq)
    ready()

    def group(t, _):
        fetched(t).wait()
        numbers = [UNROLL * t + i for i in range(UNROLL)]
        found = []
        for n in numbers:
            place = items.place(n)
            k = keys[place >> 2, span(place & (SEG - 1)), :]
            ds = ds_keep[n]
            found.append(
                [mm_tn(ds[:, h * HD : h * HD + HD], k[:, h * HD : h * HD + HD]) for h in range(2)]
            )
        for n, heads in zip(numbers, found):
            for h in range(2):
                dq[items.block(n), :, head(h)] += heads[h]
        return 0

    lax.fori_loop(0, groups, group, 0)
    for d in range(NX):
        for b in range(SEG):
            dq_out[(my_x - d) & (NX - 1), pl.ds(b * BLK, BLK), :] = dq[d * SEG + b].astype(BF16)


def far_queries(listed, me, ds, column):
    vm = pltpu.VMEM
    tiles = NX * ITEMS + UNROLL
    return call(
        far_queries_body,
        "far_queries",
        [((NX, TOK, PAIR), BF16, vm)],
        [pltpu.SMEM, pltpu.SMEM, pltpu.HBM, pltpu.HBM],
        [
            vm((NX * SEG + 1, BLK, PAIR), F32),
            vm((tiles, BLK, PAIR), BF16),
            vm((NZ, TOK, PAIR), BF16),
            pltpu.SemaphoreType.DMA((NZ,)),
            pltpu.SemaphoreType.DMA((tiles // UNROLL,)),
        ],
        2 * 2 * 16 * BLK * BLK * HD,
        6 << 20,
    )(listed, me, ds, column)[0]


def interleave(out, rows, value):
    for h in range(2):
        rows[pl.ds(h, TOK, stride=2), :] = value[:, h * HD : h * HD + HD]
    out[...] = rows[...].astype(BF16)


def near_grads_body(me, stats, qo, kv, dq_far, dq_out, kv_out, p_keep, s_keep, dq, rows_keep):
    my_x = me[0] >> 3
    tile = joined(stats, my_x, my_x)
    for h in range(2):
        k = kv[0, :, head(h)]
        for b in range(SEG):
            rows = pl.ds(b * BLK, BLK)
            p, ds = weights_of(
                qo[0, rows, head(h)], qo[1, rows, head(h)], k, kv[1, :, head(h)],
                unpacked(tile, b)[:, h * HD : h * HD + HD],
            )
            part = mm_tn(ds, k)
            for x in range(NX):
                part = part + dq_far[x, rows, head(h)].astype(F32)
            dq[rows, head(h)] = part
            p_keep[:, rows] = p
            s_keep[:, rows] = ds
        kv_out[0, :, head(h)] = mm(s_keep[...], qo[0, :, head(h)])
        kv_out[1, :, head(h)] = mm(p_keep[...], qo[1, :, head(h)])
    interleave(dq_out, rows_keep, dq[...])


def near_grads(me, stats, qo, kv, dq_far):
    vm = pltpu.VMEM
    return call(
        near_grads_body,
        "near_grads",
        [((2 * TOK, HD), BF16, vm), ((2, TOK, PAIR), F32, vm)],
        [pltpu.SMEM] + [vm] * 4,
        [
            vm((TOK, TOK), BF16),
            vm((TOK, TOK), BF16),
            vm((TOK, PAIR), F32),
            vm((2 * TOK, HD), F32),
        ],
        5 * 2 * 2 * TOK * TOK * HD,
        4 << 20,
    )(me, stats, qo, kv, dq_far)


def finish_body(near, far, dk, dv, rows):
    for s, out in enumerate((dk, dv)):
        interleave(out, rows, near[s] + far[pl.ds(s * TOK, TOK), :].astype(F32))


def finish(near, far):
    vm = pltpu.VMEM
    return call(
        finish_body,
        "finish",
        [((2 * TOK, HD), BF16, vm)] * 2,
        [vm] * 2,
        [vm((2 * TOK, HD), F32)],
        0,
        2 << 20,
    )(near, far)


def by_head_body(first, second, out, rows):
    for s, ref in enumerate((first, second)):
        rows[...] = ref[...].astype(F32)
        for h in range(2):
            out[s, :, head(h)] = rows[pl.ds(h, TOK, stride=2), :].astype(BF16)


def by_head(first, second):
    vm = pltpu.VMEM
    return call(
        by_head_body,
        "by_head",
        [((2, TOK, PAIR), BF16, vm)],
        [vm] * 2,
        [vm((2 * TOK, HD), F32)],
        0,
        1 << 20,
    )(first.reshape(2 * TOK, HD), second.reshape(2 * TOK, HD))[0]


def triangle(lower):
    i = lax.broadcasted_iota(jnp.int32, (STRETCH, STRETCH), 0)
    j = lax.broadcasted_iota(jnp.int32, (STRETCH, STRETCH), 1)
    return i >= j if lower else i <= j


def head_map(transposed):
    shape = (WIDTH, SH) if transposed else (SH, WIDTH)
    wide = lax.broadcasted_iota(jnp.int32, shape, 0 if transposed else 1)
    head = lax.broadcasted_iota(jnp.int32, shape, 1 if transposed else 0)
    return ((wide >> 6) == head).astype(BF16)


def two_part(a, b):
    high = a.astype(BF16)
    low = (a - high.astype(F32)).astype(BF16)
    return mm(high, b) + mm(low, b)


def per_head(rates, state):
    return jnp.concatenate(
        [state[h * HP : (h + 1) * HP, :] * rates[0:1, h : h + 1] for h in range(SH)], axis=0
    )


def ends_body(x_ref, g_ref, ld_ref, b_ref, c_ref, ends, starts, pay):
    lower = triangle(True).astype(F32)
    spread = head_map(False)
    last = []
    for k in range(STRETCHES):
        rows = pl.ds(k * STRETCH, STRETCH)
        cumul = dot(lower, ld_ref[rows, :], ((1,), (0,)), HIGH)
        tot = cumul[STRETCH - 1 : STRETCH, :]
        last.append(tot)
        tail = two_part(jnp.exp(tot - cumul), spread)
        lead = two_part(jnp.exp(cumul), spread)
        x_in = (x_ref[rows, :].astype(F32) * tail).astype(BF16)
        g_in = (g_ref[rows, :].astype(F32) * lead).astype(BF16)
        ends[k] = mm_tn(x_in, b_ref[rows, :])
        starts[k] = mm_tn(g_in, c_ref[rows, :])
    rates = [jnp.exp(t) for t in last]
    state = ends[0]
    for k in range(1, STRETCHES):
        state = per_head(rates[k], state) + ends[k]
    pay[:, 0:ROWS, :] = state.astype(BF16).reshape(NS, ROWS, NST)
    grad = starts[STRETCHES - 1]
    for k in range(STRETCHES - 2, -1, -1):
        grad = per_head(rates[k], grad) + starts[k]
    pay[:, ROWS : 2 * ROWS, :] = grad.astype(BF16).reshape(NS, ROWS, NST)
    whole = functools.reduce(jnp.add, last)
    high = whole.astype(BF16).astype(F32)
    low = whole - high
    line = lax.broadcasted_iota(jnp.int32, (16, NST), 0)
    for r in range(NS):
        h = r // 2
        a = jnp.broadcast_to(high[0:1, h : h + 1], (16, NST))
        b = jnp.broadcast_to(low[0:1, h : h + 1], (16, NST))
        pay[r, 2 * ROWS : PAY, :] = jnp.where(
            line == 0, a, jnp.where(line == 1, b, 0.0)
        ).astype(BF16)


def scan_ends(x, g, ld, b, c):
    vm = pltpu.VMEM
    return call(
        ends_body,
        "scan_ends",
        [
            ((STRETCHES, WIDTH, NST), F32, vm),
            ((STRETCHES, WIDTH, NST), F32, vm),
            ((NS, PAY, NST), BF16, vm),
        ],
        [vm] * 5,
        [],
        2 * 2 * TOK * WIDTH * NST * 4,
        8 << 20,
    )(x, g, ld, b, c)


def prefix_body(inp, out):
    def forward(j, state):
        out[j, 0:ROWS, :] = state.astype(BF16)
        rest = inp[j, 2 * ROWS : PAY, :].astype(F32)
        rate = jnp.exp(rest[0:1, :] + rest[1:2, :])
        return rate * state + inp[j, 0:ROWS, :].astype(F32)

    def backward(t, grad):
        j = NS - 1 - t
        out[j, ROWS : 2 * ROWS, :] = grad.astype(BF16)
        rest = inp[j, 2 * ROWS : PAY, :].astype(F32)
        rate = jnp.exp(rest[0:1, :] + rest[1:2, :])
        return rate * grad + inp[j, ROWS : 2 * ROWS, :].astype(F32)

    zero = jnp.zeros((ROWS, NST), F32)
    lax.fori_loop(0, NS, forward, zero)
    lax.fori_loop(0, NS, backward, zero)


def scan_prefix(inp):
    vm = pltpu.VMEM
    return call(
        prefix_body,
        "scan_prefix",
        [((NS, 2 * ROWS, NST), BF16, vm)],
        [vm],
        [],
        0,
        2 << 20,
    )(inp)[0]


def grads_body(
    x_ref, g_ref, ld_ref, b_ref, c_ref, ends, starts, carried, dx_ref, dl_ref, bc_ref,
    states, grads, y_keep, d_keep,
):
    lower_mask = triangle(True)
    lower = lower_mask.astype(F32)
    upper = triangle(False).astype(F32)
    spread = head_map(False)
    gathered = head_map(True)
    ones = jnp.ones((8, NST), F32)
    rates = []
    for k in range(STRETCHES):
        ld = ld_ref[pl.ds(k * STRETCH, STRETCH), :]
        rates.append(jnp.exp(jnp.sum(ld, axis=0, keepdims=True)))
    state = carried[:, 0:ROWS, :].reshape(WIDTH, NST).astype(F32)
    states[0] = state.astype(BF16)
    for k in range(STRETCHES):
        state = per_head(rates[k], state) + ends[k]
        states[k + 1] = state.astype(BF16)
    grad = carried[:, ROWS : 2 * ROWS, :].reshape(WIDTH, NST).astype(F32)
    grads[STRETCHES - 1] = grad.astype(BF16)
    for k in range(STRETCHES - 1, 0, -1):
        grad = per_head(rates[k], grad) + starts[k]
        grads[k - 1] = grad.astype(BF16)

    def stretch(k, _):
        rows = pl.ds(pl.multiple_of(k * STRETCH, STRETCH), STRETCH)
        ld = ld_ref[rows, :]
        cumul = dot(lower, ld, ((1,), (0,)), HIGH)
        cumul_t = dot(ld, upper, ((0,), (0,)), HIGH)
        tot = cumul[STRETCH - 1 : STRETCH, :]
        b = b_ref[rows, :]
        c = c_ref[rows, :]
        cb = jnp.where(lower_mask, mm_nt(c, b), 0.0)
        mixed = jnp.zeros((STRETCH, STRETCH), F32)
        for h in range(SH):
            cols = pl.ds(h * HP, HP)
            x_h = x_ref[rows, cols]
            g_h = g_ref[rows, cols]
            gap = jnp.minimum(cumul[:, h : h + 1] - cumul_t[h : h + 1, :], 0.0)
            decay = jnp.exp(gap)
            weight = (decay * cb).astype(BF16)
            mixed = mixed + decay * mm_nt(g_h, x_h)
            y_keep[:, cols] = mm(weight, x_h)
            d_keep[:, cols] = mm_tn(weight, g_h)
        mixed = jnp.where(lower_mask, mixed, 0.0).astype(BF16)
        state = states[k]
        grad = grads[k]
        lead = two_part(jnp.exp(cumul), spread)
        tail = two_part(jnp.exp(tot - cumul), spread)
        x = x_ref[rows, :].astype(F32)
        g = g_ref[rows, :].astype(F32)
        y = y_keep[...] + lead * mm_nt(c, state)
        d = d_keep[...] + tail * mm_nt(b, grad)
        dx_ref[rows, :] = d.astype(BF16)
        bc_ref[rows, :] = (mm_tn(mixed, c) + mm((tail * x).astype(BF16), grad)).astype(BF16)
        c_rows = pl.ds(pl.multiple_of(TOK + k * STRETCH, STRETCH), STRETCH)
        bc_ref[c_rows, :] = (mm(mixed, b) + mm((lead * g).astype(BF16), state)).astype(BF16)
        change = two_part(g * y - x * d, gathered)
        meet = grad.astype(F32) * states[k + 1].astype(F32)
        meet = jnp.sum(meet.reshape(SH, HP, NST), axis=1)
        edge = dot(ones, meet, ((1,), (1,)), HIGH)[0:1, :]
        dl_ref[rows, :] = dot(upper, change, ((1,), (0,)), HIGH) + edge
        return 0

    lax.fori_loop(0, STRETCHES, stretch, 0)


def scan_grads(x, g, ld, b, c, ends, starts, carried):
    vm = pltpu.VMEM
    return call(
        grads_body,
        "scan_grads",
        [
            ((TOK, WIDTH), BF16, vm),
            ((TOK, SH), F32, vm),
            ((2 * TOK, NST), BF16, vm),
        ],
        [vm] * 8,
        [
            vm((STRETCHES + 1, WIDTH, NST), BF16),
            vm((STRETCHES, WIDTH, NST), BF16),
            vm((STRETCH, WIDTH), F32),
            vm((STRETCH, WIDTH), F32),
        ],
        2 * 8 * TOK * WIDTH * NST * 4,
        12 << 20,
    )(x, g, ld, b, c, ends, starts, carried)


def exchange(value, groups=None):
    return lax.all_to_all(value, "seq", 0, 0, tiled=True, axis_index_groups=groups)


def along_x(value, step):
    pairs = [
        (x * NZ + z, (x + step) % NX * NZ + z) for x in range(NX) for z in range(NZ)
    ]
    return lax.ppermute(value, "seq", pairs)


def after(value, *earlier):
    return lax.optimization_barrier((value, earlier))[0]


def per_device(q, k, v, o, x, ld, b, c, g, owner, offset, count):
    me = lax.axis_index("seq").astype(jnp.int32).reshape(1)
    kv = by_head(k, v)
    column = lax.all_gather(kv, "seq", axis_index_groups=Z_GROUPS)
    qo = by_head(q, o)
    live = jnp.arange(GLOB)[None, :] < count[:, None]
    codes = jnp.where(live, owner * SEG + offset, -1).reshape(NS * ITEMS)
    listed = far_items(codes, me)
    shifted = [along_x(qo, 1), along_x(qo, 3)]
    opposite = jnp.concatenate([along_x(shifted[0][:1], 1), along_x(shifted[1][1:], 3)])
    qos = jnp.stack([qo, shifted[0], opposite, shifted[1]])
    near = near_stats(qo, kv)
    ends, starts, pay = scan_ends(x, g, ld, b, c)
    pay = exchange(after(pay, shifted[0], shifted[1], near, listed))
    carried = scan_prefix(pay)
    column = after(column, qos)
    carried = exchange(after(carried, column))
    stats = far_stats(listed, near, column, qos)
    stats = jnp.stack([stats] + [along_x(stats, d) for d in range(1, NX)])
    kv_far, ds_far = far_grads(listed, me, stats, column, qos)
    kv_far = lax.psum_scatter(
        after(kv_far, carried), "seq", scatter_dimension=0, axis_index_groups=Z_GROUPS
    )
    dq_far = far_queries(listed, me, ds_far, column)
    dx, dl, bc = scan_grads(x, g, ld, b, c, ends, starts, carried)
    shares = lax.all_to_all(bc.reshape(8, 128, NST), "head", 0, 0, tiled=True)
    dq_far = exchange(after(dq_far, bc), X_GROUPS)
    part = jnp.sum(shares.astype(F32), axis=0).astype(BF16)
    whole = lax.all_gather(part, "head", tiled=True).astype(F32)
    dq, kv_near = near_grads(me, stats, qo, kv, dq_far)
    dk, dv = finish(kv_near, kv_far)
    return (
        dq.reshape(q.shape),
        dk.reshape(k.shape),
        dv.reshape(v.shape),
        dx,
        dl,
        whole[:TOK],
        whole[TOK:],
    )


def solution(mesh):
    wide = P("seq", "head", None)
    flat = P("seq", "head")
    own = P("seq", None)
    return jax.shard_map(
        per_device,
        mesh=mesh,
        in_specs=(wide, wide, wide, wide, flat, flat, own, own, flat, P(), P(), P()),
        out_specs=(wide, wide, wide, flat, flat, own, own),
        check_vma=False,
    )
```

```python
import functools
import math

import jax
import jax.numpy as jnp
from jax import lax
from jax.experimental import pallas as pl
from jax.experimental.pallas import tpu as pltpu
from jax.sharding import PartitionSpec as P

HD = 128
HP = 64
NST = 128
BLK = 128
STRETCH = 128
SEG = 4
GLOB = 4
TOK = 512
SH = 16
WIDTH = SH * HP
ITEMS = SEG * GLOB
NX = 4
NZ = 8
NS = NX * NZ
ROWS = WIDTH // NS
PAY = 2 * ROWS + 16
STRETCHES = TOK // STRETCH

HIGH = lax.Precision.HIGHEST
F32 = jnp.float32
BF16 = jnp.bfloat16
Z_GROUPS = [[x * NZ + z for z in range(NZ)] for x in range(NX)]
X_GROUPS = [[x * NZ + z for x in range(NX)] for z in range(NZ)]


def dot(a, b, dims, precision=None):
    return lax.dot_general(
        a, b, (dims, ((), ())), precision=precision, preferred_element_type=F32
    )


def mm(a, b):
    return dot(a, b, ((1,), (0,)))


def mm_nt(a, b):
    return dot(a, b, ((1,), (1,)))


def mm_tn(a, b):
    return dot(a, b, ((0,), (0,)))


def call(body, name, outs, ins, scratch, flops, nbytes, vmem=48 << 20):
    return pl.pallas_call(
        body,
        out_shape=[jax.ShapeDtypeStruct(s, d) for s, d, _ in outs],
        in_specs=[pl.BlockSpec(memory_space=m) for m in ins],
        out_specs=[pl.BlockSpec(memory_space=m) for _, _, m in outs],
        scratch_shapes=scratch,
        compiler_params=pltpu.CompilerParams(vmem_limit_bytes=vmem),
        cost_estimate=pl.CostEstimate(flops=flops, bytes_accessed=nbytes, transcendentals=0),
        name=name,
    )


SCALE = 1.0 / math.sqrt(HD)
EMPTY = -1e30
KINDS = 3
FAR = NZ * SEG
UNROLL = 4
PAIR = 2 * HD


def far_items(codes, me):
    my_x = me[0] >> 3
    my_z = me[0] & (NZ - 1)
    sources = ((my_x - jnp.arange(NX)) & (NX - 1)) * NZ + my_z
    code = jnp.take(codes.reshape(NS, ITEMS), sources, axis=0).reshape(NX * ITEMS)
    block = jnp.arange(NX * ITEMS) // GLOB
    hit = (code >= 0) & ((code >> 5) == my_x)
    order = jnp.arange(NX * ITEMS)
    rank = jnp.sum((hit[None, :] & (order[None, :] < order[:, None])).astype(jnp.int32), axis=1)
    slot = jnp.arange(NX * ITEMS + UNROLL)[:, None]
    chosen = hit[None, :] & (rank[None, :] == slot)
    places = jnp.sum(jnp.where(chosen, code[None, :] & (FAR - 1), 0), axis=1)
    blocks = NX * SEG + jnp.sum(jnp.where(chosen, block[None, :] - NX * SEG, 0), axis=1)
    count = jnp.sum(hit.astype(jnp.int32)).reshape(1)
    return jnp.concatenate([count, places, blocks]).astype(jnp.int32)


class Listed:
    def __init__(self, ref):
        self.count = ref[0]
        self.place = lambda n: ref[1 + n]
        self.block = lambda n: ref[1 + NX * ITEMS + UNROLL + n]


def span(index):
    return pl.ds(pl.multiple_of(index * BLK, BLK), BLK)


def in_groups(count, visit):
    def group(t, _):
        visit([UNROLL * t + i for i in range(UNROLL)])
        return 0

    lax.fori_loop(0, (count + UNROLL - 1) // UNROLL, group, 0)


def head(h):
    return pl.ds(h * HD, HD)


def summary(q, o, k, v):
    s = mm_nt(k, q) * SCALE
    dp = mm_nt(v, o)
    m = jnp.max(s, axis=0, keepdims=True)
    e = jnp.exp(s - m)
    return [m, jnp.sum(e, axis=0, keepdims=True), jnp.sum(e * dp, axis=0, keepdims=True)]


def packed(quads):
    return jnp.concatenate(
        [jnp.concatenate([quads[i], quads[i + 2]], axis=0) for i in range(2)], axis=1
    )


def unpacked(tile, b):
    at = 4 * (b >> 1)
    return tile[at : at + KINDS, (b & 1) * PAIR : (b & 1) * PAIR + PAIR]


def near_stats_body(qo, kv, out):
    quads = []
    for b in range(SEG):
        rows = pl.ds(b * BLK, BLK)
        heads = [
            summary(qo[0, rows, head(h)], qo[1, rows, head(h)], kv[0, :, head(h)], kv[1, :, head(h)])
            for h in range(2)
        ]
        quads.append(
            jnp.concatenate(
                [jnp.concatenate([x, y], axis=1) for x, y in zip(*heads)]
                + [jnp.zeros((1, PAIR), F32)],
                axis=0,
            )
        )
    out[...] = packed(quads)


def near_stats(qo, kv):
    vm = pltpu.VMEM
    return call(
        near_stats_body,
        "near_stats",
        [((8, 2 * PAIR), F32, vm)],
        [vm, vm],
        [],
        2 * 2 * 2 * TOK * TOK * HD,
        1 << 20,
    )(qo, kv)[0]


def spread(value):
    lane = lax.broadcasted_iota(jnp.int32, (BLK, PAIR), 1)
    zero = jnp.zeros((BLK, PAIR), BF16)
    return jnp.concatenate(
        [jnp.where(lane < HD, value, zero), jnp.where(lane < HD, zero, value)], axis=0
    )


def load(pieces, sems):
    copies = [pltpu.make_async_copy(a, b, sems.at[i]) for i, (a, b) in enumerate(pieces)]
    for copy in copies:
        copy.start()

    def wait():
        for copy in copies:
            copy.wait()

    return wait


def load_far(column_in, qos_in, column, qos, sems):
    return load(
        [(column_in.at[z], column.at[z]) for z in range(NZ)]
        + [(qos_in.at[d], qos.at[d]) for d in range(NX)],
        sems,
    )


def far_scratch():
    return [
        pltpu.VMEM((NZ, 2, TOK, PAIR), BF16),
        pltpu.VMEM((NX, 2, TOK, PAIR), BF16),
        pltpu.SemaphoreType.DMA((NZ + NX,)),
    ]


def fetch(qos, keys, place, block):
    n = jnp.minimum(block, NX * SEG - 1)
    d = n >> 2
    rows = span(n & (SEG - 1))
    z = place >> 2
    cols = span(place & (SEG - 1))
    return (
        spread(qos[d, 0, rows, :]), spread(qos[d, 1, rows, :]), keys[z, 0, cols, :], keys[z, 1, cols, :]
    )


def far_stats_body(listed, near, column_in, qos_in, out, tally, column, qos, sems):
    ready = load_far(column_in, qos_in, column, qos, sems)
    items = Listed(listed)
    kind = lax.broadcasted_iota(jnp.int32, (4, PAIR), 0)
    start = jnp.where(kind == 0, EMPTY, 0.0)
    for n in range(NX * SEG + 1):
        tally[n] = start
    ready()

    def visit(numbers):
        found = [summary(*fetch(qos, column, items.place(n), items.block(n))) for n in numbers]
        for n, (m, l, t) in zip(numbers, found):
            old = tally[items.block(n)]
            m0, l0, t0 = [old[i : i + 1, :] for i in range(KINDS)]
            high = jnp.maximum(m0, m)
            f0 = jnp.exp(m0 - high)
            f1 = jnp.exp(m - high)
            tally[items.block(n)] = jnp.concatenate(
                [high, l0 * f0 + l * f1, t0 * f0 + t * f1, jnp.zeros_like(high)], axis=0
            )

    in_groups(items.count, visit)
    for d in range(NX):
        out[d] = packed([tally[d * SEG + b] for b in range(SEG)])
    out[NX] = near[...]


def far_stats(listed, near, column, qos):
    vm = pltpu.VMEM
    return call(
        far_stats_body,
        "far_stats",
        [((NX + 1, 8, 2 * PAIR), F32, vm)],
        [pltpu.SMEM, vm, pltpu.HBM, pl.ANY],
        [vm((NX * SEG + 1, 4, PAIR), F32)] + far_scratch(),
        2 * 2 * 2 * 16 * BLK * BLK * HD,
        6 << 20,
    )(listed, near, column, qos)[0]


def joined(stats, my_x, x_q):
    parts = []
    for r in range(NX):
        x = (my_x - r) & (NX - 1)
        parts.append(stats[r, (x - x_q) & (NX - 1)])
    parts.append(stats[(my_x - x_q) & (NX - 1), NX])
    rows = []
    for at in (0, 4):
        high = functools.reduce(jnp.maximum, [p[at : at + 1, :] for p in parts])
        fade = [jnp.exp(p[at : at + 1, :] - high) for p in parts]
        total = sum(f * p[at + 1 : at + 2, :] for f, p in zip(fade, parts))
        mixed = sum(f * p[at + 2 : at + 3, :] for f, p in zip(fade, parts))
        inverse = 1.0 / total
        rows += [high, inverse, mixed * inverse, jnp.zeros_like(high)]
    return jnp.concatenate(rows, axis=0)


def weights_of(q, o, k, v, row):
    high, inverse, delta = [row[i : i + 1, :] for i in range(KINDS)]
    p = jnp.exp(mm_nt(k, q) * SCALE - high) * inverse
    ds = (p * (mm_nt(v, o) - delta) * SCALE).astype(BF16)
    return p.astype(BF16), ds


def ds_copies(a, b, sems):
    def group(t):
        tiles = pl.ds(UNROLL * t, UNROLL)
        return pltpu.make_async_copy(a.at[tiles], b.at[tiles], sems.at[t])

    return group


def far_grads_body(
    listed, me, stats, column_in, qos_in, kv_out, ds_out,
    total, rowed, staged, ds_keep, column, qos, sems, out_sems, ds_sems,
):
    ready = load_far(column_in, qos_in, column, qos, sems)
    my_x = me[0] >> 3
    items = Listed(listed)
    sent = ds_copies(ds_keep, ds_out, ds_sems)
    total[...] = jnp.zeros_like(total)
    for d in range(NX):
        tile = joined(stats, my_x, (my_x - d) & (NX - 1))
        for b in range(SEG):
            rowed[d * SEG + b, 0:KINDS, :] = unpacked(tile, b)
    rowed[NX * SEG] = jnp.zeros((8, PAIR), F32)
    ready()

    def group(t, _):
        numbers = [UNROLL * t + i for i in range(UNROLL)]
        found = []
        for n in numbers:
            q, o, k, v = fetch(qos, column, items.place(n), items.block(n))
            p, ds = weights_of(q, o, k, v, rowed[items.block(n)])
            found.append((ds, mm(ds, q), mm(p, o)))
        for n, (ds, dk, dv) in zip(numbers, found):
            to = jnp.where(items.block(n) == NX * SEG, FAR, items.place(n))
            ds_keep[n] = ds
            total[to, 0] += dk
            total[to, 1] += dv
        sent(t).start()
        return 0

    groups = (items.count + UNROLL - 1) // UNROLL
    lax.fori_loop(0, groups, group, 0)
    copies = []
    for z in range(NZ):
        for s in range(2):
            for b in range(SEG):
                staged[z, pl.ds(s * TOK + b * BLK, BLK), :] = total[z * SEG + b, s].astype(BF16)
        copies.append(pltpu.make_async_copy(staged.at[z], kv_out.at[z], out_sems.at[z]))
        copies[-1].start()

    def drain(t, _):
        sent(t).wait()
        return 0

    lax.fori_loop(0, groups, drain, 0)
    for copy in copies:
        copy.wait()


def far_grads(listed, me, stats, column, qos):
    vm = pltpu.VMEM
    tiles = NX * ITEMS + UNROLL
    return call(
        far_grads_body,
        "far_grads",
        [
            ((NZ, 2 * TOK, PAIR), BF16, pltpu.HBM),
            ((tiles, BLK, PAIR), BF16, pltpu.HBM),
        ],
        [pltpu.SMEM, pltpu.SMEM, vm, pltpu.HBM, pl.ANY],
        [
            vm((FAR + 1, 2, BLK, PAIR), F32),
            vm((NX * SEG + 1, 8, PAIR), F32),
            vm((NZ, 2 * TOK, PAIR), BF16),
            vm((tiles, BLK, PAIR), BF16),
        ]
        + far_scratch()
        + [pltpu.SemaphoreType.DMA((NZ,)), pltpu.SemaphoreType.DMA((tiles // UNROLL,))],
        4 * 2 * 2 * 16 * BLK * BLK * HD,
        12 << 20,
    )(listed, me, stats, column, qos)


def far_queries_body(listed, me, ds_in, column_in, dq_out, dq, ds_keep, keys, sems, ds_sems):
    ready = load([(column_in.at[z, 0], keys.at[z]) for z in range(NZ)], sems)
    my_x = me[0] >> 3
    items = Listed(listed)
    fetched = ds_copies(ds_in, ds_keep, ds_sems)
    groups = (items.count + UNROLL - 1) // UNROLL

    def begin(t, _):
        fetched(t).start()
        return 0

    lax.fori_loop(0, groups, begin, 0)
    dq[...] = jnp.zeros_like(dq)
    ready()

    def group(t, _):
        fetched(t).wait()
        numbers = [UNROLL * t + i for i in range(UNROLL)]
        found = []
        for n in numbers:
            place = items.place(n)
            k = keys[place >> 2, span(place & (SEG - 1)), :]
            ds = ds_keep[n]
            found.append(
                [mm_tn(ds[:, h * HD : h * HD + HD], k[:, h * HD : h * HD + HD]) for h in range(2)]
            )
        for n, heads in zip(numbers, found):
            for h in range(2):
                dq[items.block(n), :, head(h)] += heads[h]
        return 0

    lax.fori_loop(0, groups, group, 0)
    for d in range(NX):
        for b in range(SEG):
            dq_out[(my_x - d) & (NX - 1), pl.ds(b * BLK, BLK), :] = dq[d * SEG + b].astype(BF16)


def far_queries(listed, me, ds, column):
    vm = pltpu.VMEM
    tiles = NX * ITEMS + UNROLL
    return call(
        far_queries_body,
        "far_queries",
        [((NX, TOK, PAIR), BF16, vm)],
        [pltpu.SMEM, pltpu.SMEM, pltpu.HBM, pltpu.HBM],
        [
            vm((NX * SEG + 1, BLK, PAIR), F32),
            vm((tiles, BLK, PAIR), BF16),
            vm((NZ, TOK, PAIR), BF16),
            pltpu.SemaphoreType.DMA((NZ,)),
            pltpu.SemaphoreType.DMA((tiles // UNROLL,)),
        ],
        2 * 2 * 16 * BLK * BLK * HD,
        6 << 20,
    )(listed, me, ds, column)[0]


def interleave(out, rows, value):
    for h in range(2):
        rows[pl.ds(h, TOK, stride=2), :] = value[:, h * HD : h * HD + HD]
    out[...] = rows[...].astype(BF16)


def near_grads_body(me, stats, qo, kv, dq_far, dq_out, kv_out, p_keep, s_keep, dq, rows_keep):
    my_x = me[0] >> 3
    tile = joined(stats, my_x, my_x)
    for h in range(2):
        k = kv[0, :, head(h)]
        for b in range(SEG):
            rows = pl.ds(b * BLK, BLK)
            p, ds = weights_of(
                qo[0, rows, head(h)], qo[1, rows, head(h)], k, kv[1, :, head(h)],
                unpacked(tile, b)[:, h * HD : h * HD + HD],
            )
            part = mm_tn(ds, k)
            for x in range(NX):
                part = part + dq_far[x, rows, head(h)].astype(F32)
            dq[rows, head(h)] = part
            p_keep[:, rows] = p
            s_keep[:, rows] = ds
        kv_out[0, :, head(h)] = mm(s_keep[...], qo[0, :, head(h)])
        kv_out[1, :, head(h)] = mm(p_keep[...], qo[1, :, head(h)])
    interleave(dq_out, rows_keep, dq[...])


def near_grads(me, stats, qo, kv, dq_far):
    vm = pltpu.VMEM
    return call(
        near_grads_body,
        "near_grads",
        [((2 * TOK, HD), BF16, vm), ((2, TOK, PAIR), F32, vm)],
        [pltpu.SMEM] + [vm] * 4,
        [
            vm((TOK, TOK), BF16),
            vm((TOK, TOK), BF16),
            vm((TOK, PAIR), F32),
            vm((2 * TOK, HD), F32),
        ],
        5 * 2 * 2 * TOK * TOK * HD,
        4 << 20,
    )(me, stats, qo, kv, dq_far)


def finish_body(near, far, dk, dv, rows):
    for s, out in enumerate((dk, dv)):
        interleave(out, rows, near[s] + far[pl.ds(s * TOK, TOK), :].astype(F32))


def finish(near, far):
    vm = pltpu.VMEM
    return call(
        finish_body,
        "finish",
        [((2 * TOK, HD), BF16, vm)] * 2,
        [vm] * 2,
        [vm((2 * TOK, HD), F32)],
        0,
        2 << 20,
    )(near, far)


def by_head_body(first, second, out, rows):
    for s, ref in enumerate((first, second)):
        rows[...] = ref[...].astype(F32)
        for h in range(2):
            out[s, :, head(h)] = rows[pl.ds(h, TOK, stride=2), :].astype(BF16)


def by_head(first, second):
    vm = pltpu.VMEM
    return call(
        by_head_body,
        "by_head",
        [((2, TOK, PAIR), BF16, vm)],
        [vm] * 2,
        [vm((2 * TOK, HD), F32)],
        0,
        1 << 20,
    )(first.reshape(2 * TOK, HD), second.reshape(2 * TOK, HD))[0]


def triangle(lower):
    i = lax.broadcasted_iota(jnp.int32, (STRETCH, STRETCH), 0)
    j = lax.broadcasted_iota(jnp.int32, (STRETCH, STRETCH), 1)
    return i >= j if lower else i <= j


def head_map(transposed):
    shape = (WIDTH, SH) if transposed else (SH, WIDTH)
    wide = lax.broadcasted_iota(jnp.int32, shape, 0 if transposed else 1)
    head = lax.broadcasted_iota(jnp.int32, shape, 1 if transposed else 0)
    return ((wide >> 6) == head).astype(BF16)


def two_part(a, b):
    high = a.astype(BF16)
    low = (a - high.astype(F32)).astype(BF16)
    return mm(high, b) + mm(low, b)


def per_head(rates, state):
    return jnp.concatenate(
        [state[h * HP : (h + 1) * HP, :] * rates[0:1, h : h + 1] for h in range(SH)], axis=0
    )


def ends_body(x_ref, g_ref, ld_ref, b_ref, c_ref, ends, starts, pay):
    lower = triangle(True).astype(F32)
    spread = head_map(False)
    last = []
    for k in range(STRETCHES):
        rows = pl.ds(k * STRETCH, STRETCH)
        cumul = dot(lower, ld_ref[rows, :], ((1,), (0,)), HIGH)
        tot = cumul[STRETCH - 1 : STRETCH, :]
        last.append(tot)
        tail = two_part(jnp.exp(tot - cumul), spread)
        lead = two_part(jnp.exp(cumul), spread)
        x_in = (x_ref[rows, :].astype(F32) * tail).astype(BF16)
        g_in = (g_ref[rows, :].astype(F32) * lead).astype(BF16)
        ends[k] = mm_tn(x_in, b_ref[rows, :])
        starts[k] = mm_tn(g_in, c_ref[rows, :])
    rates = [jnp.exp(t) for t in last]
    state = ends[0]
    for k in range(1, STRETCHES):
        state = per_head(rates[k], state) + ends[k]
    pay[:, 0:ROWS, :] = state.astype(BF16).reshape(NS, ROWS, NST)
    grad = starts[STRETCHES - 1]
    for k in range(STRETCHES - 2, -1, -1):
        grad = per_head(rates[k], grad) + starts[k]
    pay[:, ROWS : 2 * ROWS, :] = grad.astype(BF16).reshape(NS, ROWS, NST)
    whole = functools.reduce(jnp.add, last)
    high = whole.astype(BF16).astype(F32)
    low = whole - high
    line = lax.broadcasted_iota(jnp.int32, (16, NST), 0)
    for r in range(NS):
        h = r // 2
        a = jnp.broadcast_to(high[0:1, h : h + 1], (16, NST))
        b = jnp.broadcast_to(low[0:1, h : h + 1], (16, NST))
        pay[r, 2 * ROWS : PAY, :] = jnp.where(
            line == 0, a, jnp.where(line == 1, b, 0.0)
        ).astype(BF16)


def scan_ends(x, g, ld, b, c):
    vm = pltpu.VMEM
    return call(
        ends_body,
        "scan_ends",
        [
            ((STRETCHES, WIDTH, NST), F32, vm),
            ((STRETCHES, WIDTH, NST), F32, vm),
            ((NS, PAY, NST), BF16, vm),
        ],
        [vm] * 5,
        [],
        2 * 2 * TOK * WIDTH * NST * 4,
        8 << 20,
    )(x, g, ld, b, c)


def prefix_body(inp, out):
    def forward(j, state):
        out[j, 0:ROWS, :] = state.astype(BF16)
        rest = inp[j, 2 * ROWS : PAY, :].astype(F32)
        rate = jnp.exp(rest[0:1, :] + rest[1:2, :])
        return rate * state + inp[j, 0:ROWS, :].astype(F32)

    def backward(t, grad):
        j = NS - 1 - t
        out[j, ROWS : 2 * ROWS, :] = grad.astype(BF16)
        rest = inp[j, 2 * ROWS : PAY, :].astype(F32)
        rate = jnp.exp(rest[0:1, :] + rest[1:2, :])
        return rate * grad + inp[j, ROWS : 2 * ROWS, :].astype(F32)

    zero = jnp.zeros((ROWS, NST), F32)
    lax.fori_loop(0, NS, forward, zero)
    lax.fori_loop(0, NS, backward, zero)


def scan_prefix(inp):
    vm = pltpu.VMEM
    return call(
        prefix_body,
        "scan_prefix",
        [((NS, 2 * ROWS, NST), BF16, vm)],
        [vm],
        [],
        0,
        2 << 20,
    )(inp)[0]


def grads_body(
    x_ref, g_ref, ld_ref, b_ref, c_ref, ends, starts, carried, dx_ref, dl_ref, bc_ref,
    states, grads, y_keep, d_keep,
):
    lower_mask = triangle(True)
    lower = lower_mask.astype(F32)
    upper = triangle(False).astype(F32)
    spread = head_map(False)
    gathered = head_map(True)
    ones = jnp.ones((8, NST), F32)
    rates = []
    for k in range(STRETCHES):
        ld = ld_ref[pl.ds(k * STRETCH, STRETCH), :]
        rates.append(jnp.exp(jnp.sum(ld, axis=0, keepdims=True)))
    state = carried[:, 0:ROWS, :].reshape(WIDTH, NST).astype(F32)
    states[0] = state.astype(BF16)
    for k in range(STRETCHES):
        state = per_head(rates[k], state) + ends[k]
        states[k + 1] = state.astype(BF16)
    grad = carried[:, ROWS : 2 * ROWS, :].reshape(WIDTH, NST).astype(F32)
    grads[STRETCHES - 1] = grad.astype(BF16)
    for k in range(STRETCHES - 1, 0, -1):
        grad = per_head(rates[k], grad) + starts[k]
        grads[k - 1] = grad.astype(BF16)

    def stretch(k, _):
        rows = pl.ds(pl.multiple_of(k * STRETCH, STRETCH), STRETCH)
        ld = ld_ref[rows, :]
        cumul = dot(lower, ld, ((1,), (0,)), HIGH)
        cumul_t = dot(ld, upper, ((0,), (0,)), HIGH)
        tot = cumul[STRETCH - 1 : STRETCH, :]
        b = b_ref[rows, :]
        c = c_ref[rows, :]
        cb = jnp.where(lower_mask, mm_nt(c, b), 0.0)
        mixed = jnp.zeros((STRETCH, STRETCH), F32)
        for h in range(SH):
            cols = pl.ds(h * HP, HP)
            x_h = x_ref[rows, cols]
            g_h = g_ref[rows, cols]
            gap = jnp.minimum(cumul[:, h : h + 1] - cumul_t[h : h + 1, :], 0.0)
            decay = jnp.exp(gap)
            weight = (decay * cb).astype(BF16)
            mixed = mixed + decay * mm_nt(g_h, x_h)
            y_keep[:, cols] = mm(weight, x_h)
            d_keep[:, cols] = mm_tn(weight, g_h)
        mixed = jnp.where(lower_mask, mixed, 0.0).astype(BF16)
        state = states[k]
        grad = grads[k]
        lead = two_part(jnp.exp(cumul), spread)
        tail = two_part(jnp.exp(tot - cumul), spread)
        x = x_ref[rows, :].astype(F32)
        g = g_ref[rows, :].astype(F32)
        y = y_keep[...] + lead * mm_nt(c, state)
        d = d_keep[...] + tail * mm_nt(b, grad)
        dx_ref[rows, :] = d.astype(BF16)
        bc_ref[rows, :] = (mm_tn(mixed, c) + mm((tail * x).astype(BF16), grad)).astype(BF16)
        c_rows = pl.ds(pl.multiple_of(TOK + k * STRETCH, STRETCH), STRETCH)
        bc_ref[c_rows, :] = (mm(mixed, b) + mm((lead * g).astype(BF16), state)).astype(BF16)
        change = two_part(g * y - x * d, gathered)
        meet = grad.astype(F32) * states[k + 1].astype(F32)
        meet = jnp.sum(meet.reshape(SH, HP, NST), axis=1)
        edge = dot(ones, meet, ((1,), (1,)), HIGH)[0:1, :]
        dl_ref[rows, :] = dot(upper, change, ((1,), (0,)), HIGH) + edge
        return 0

    lax.fori_loop(0, STRETCHES, stretch, 0)


def scan_grads(x, g, ld, b, c, ends, starts, carried):
    vm = pltpu.VMEM
    return call(
        grads_body,
        "scan_grads",
        [
            ((TOK, WIDTH), BF16, vm),
            ((TOK, SH), F32, vm),
            ((2 * TOK, NST), BF16, vm),
        ],
        [vm] * 8,
        [
            vm((STRETCHES + 1, WIDTH, NST), BF16),
            vm((STRETCHES, WIDTH, NST), BF16),
            vm((STRETCH, WIDTH), F32),
            vm((STRETCH, WIDTH), F32),
        ],
        2 * 8 * TOK * WIDTH * NST * 4,
        12 << 20,
    )(x, g, ld, b, c, ends, starts, carried)


def exchange(value, groups=None):
    return lax.all_to_all(value, "seq", 0, 0, tiled=True, axis_index_groups=groups)


def along_x(value, step):
    pairs = [
        (x * NZ + z, (x + step) % NX * NZ + z) for x in range(NX) for z in range(NZ)
    ]
    return lax.ppermute(value, "seq", pairs)


def after(value, *earlier):
    return lax.optimization_barrier((value, earlier))[0]


def per_device(q, k, v, o, x, ld, b, c, g, owner, offset, count):
    me = lax.axis_index("seq").astype(jnp.int32).reshape(1)
    kv = by_head(k, v)
    column = lax.all_gather(kv, "seq", axis_index_groups=Z_GROUPS)
    qo = by_head(q, o)
    live = jnp.arange(GLOB)[None, :] < count[:, None]
    codes = jnp.where(live, owner * SEG + offset, -1).reshape(NS * ITEMS)
    shifted = [along_x(qo, 1), along_x(qo, 3)]
    opposite = [along_x(shifted[0][:1], 1), along_x(shifted[1][1:], 3)]
    ends, starts, pay = scan_ends(x, g, ld, b, c)
    pay = exchange(after(pay, shifted[0], shifted[1]))
    listed = far_items(after(codes, pay), me)
    opposite = jnp.concatenate(after(opposite, pay))
    qos = jnp.stack([qo, shifted[0], opposite, shifted[1]])
    near = near_stats(after(qo, pay), kv)
    carried = exchange(scan_prefix(after(pay, near, listed, qos)))
    stats = far_stats(listed, near, column, qos)
    stats = jnp.stack([stats] + [along_x(stats, d) for d in range(1, NX)])
    kv_far, ds_far = far_grads(listed, me, stats, column, qos)
    kv_far = lax.psum_scatter(
        after(kv_far, carried), "seq", scatter_dimension=0, axis_index_groups=Z_GROUPS
    )
    dq_far = far_queries(listed, me, ds_far, column)
    dx, dl, bc = scan_grads(x, g, ld, b, c, ends, starts, carried)
    shares = lax.all_to_all(bc.reshape(8, 128, NST), "head", 0, 0, tiled=True)
    dq_far = exchange(after(dq_far, bc), X_GROUPS)
    part = jnp.sum(shares.astype(F32), axis=0).astype(BF16)
    whole = lax.all_gather(part, "head", tiled=True).astype(F32)
    dq, kv_near = near_grads(me, stats, qo, kv, dq_far)
    dk, dv = finish(kv_near, kv_far)
    return (
        dq.reshape(q.shape),
        dk.reshape(k.shape),
        dv.reshape(v.shape),
        dx,
        dl,
        whole[:TOK],
        whole[TOK:],
    )


def solution(mesh):
    wide = P("seq", "head", None)
    flat = P("seq", "head")
    own = P("seq", None)
    return jax.shard_map(
        per_device,
        mesh=mesh,
        in_specs=(wide, wide, wide, wide, flat, flat, own, own, flat, P(), P(), P()),
        out_specs=(wide, wide, wide, flat, flat, own, own),
        check_vma=False,
    )
```

```python
import functools
import math

import jax
import jax.numpy as jnp
from jax import lax
from jax.experimental import pallas as pl
from jax.experimental.pallas import tpu as pltpu
from jax.sharding import PartitionSpec as P

HD = 128
HP = 64
NST = 128
BLK = 128
STRETCH = 128
SEG = 4
GLOB = 4
TOK = 512
SH = 16
WIDTH = SH * HP
ITEMS = SEG * GLOB
NX = 4
NZ = 8
NS = NX * NZ
ROWS = WIDTH // NS
PAY = 2 * ROWS + 16
STRETCHES = TOK // STRETCH

HIGH = lax.Precision.HIGHEST
F32 = jnp.float32
BF16 = jnp.bfloat16
Z_GROUPS = [[x * NZ + z for z in range(NZ)] for x in range(NX)]
X_GROUPS = [[x * NZ + z for x in range(NX)] for z in range(NZ)]


def dot(a, b, dims, precision=None):
    return lax.dot_general(
        a, b, (dims, ((), ())), precision=precision, preferred_element_type=F32
    )


def mm(a, b):
    return dot(a, b, ((1,), (0,)))


def mm_nt(a, b):
    return dot(a, b, ((1,), (1,)))


def mm_tn(a, b):
    return dot(a, b, ((0,), (0,)))


def call(body, name, outs, ins, scratch, flops, nbytes, vmem=48 << 20):
    return pl.pallas_call(
        body,
        out_shape=[jax.ShapeDtypeStruct(s, d) for s, d, _ in outs],
        in_specs=[pl.BlockSpec(memory_space=m) for m in ins],
        out_specs=[pl.BlockSpec(memory_space=m) for _, _, m in outs],
        scratch_shapes=scratch,
        compiler_params=pltpu.CompilerParams(vmem_limit_bytes=vmem),
        cost_estimate=pl.CostEstimate(flops=flops, bytes_accessed=nbytes, transcendentals=0),
        name=name,
    )


SCALE = 1.0 / math.sqrt(HD)
EMPTY = -1e30
KINDS = 3
FAR = NZ * SEG
UNROLL = 4
PAIR = 2 * HD


def far_items(codes, me):
    my_x = me[0] >> 3
    my_z = me[0] & (NZ - 1)
    sources = ((my_x - jnp.arange(NX)) & (NX - 1)) * NZ + my_z
    code = jnp.take(codes.reshape(NS, ITEMS), sources, axis=0).reshape(NX * ITEMS)
    block = jnp.arange(NX * ITEMS) // GLOB
    hit = (code >= 0) & ((code >> 5) == my_x)
    order = jnp.arange(NX * ITEMS)
    rank = jnp.sum((hit[None, :] & (order[None, :] < order[:, None])).astype(jnp.int32), axis=1)
    slot = jnp.arange(NX * ITEMS + UNROLL)[:, None]
    chosen = hit[None, :] & (rank[None, :] == slot)
    places = jnp.sum(jnp.where(chosen, code[None, :] & (FAR - 1), 0), axis=1)
    blocks = NX * SEG + jnp.sum(jnp.where(chosen, block[None, :] - NX * SEG, 0), axis=1)
    count = jnp.sum(hit.astype(jnp.int32)).reshape(1)
    return jnp.concatenate([count, places, blocks]).astype(jnp.int32)


class Listed:
    def __init__(self, ref):
        self.count = ref[0]
        self.place = lambda n: ref[1 + n]
        self.block = lambda n: ref[1 + NX * ITEMS + UNROLL + n]


def span(index):
    return pl.ds(pl.multiple_of(index * BLK, BLK), BLK)


def in_groups(count, visit):
    def group(t, _):
        visit([UNROLL * t + i for i in range(UNROLL)])
        return 0

    lax.fori_loop(0, (count + UNROLL - 1) // UNROLL, group, 0)


def head(h):
    return pl.ds(h * HD, HD)


def summary(q, o, k, v):
    s = mm_nt(k, q) * SCALE
    dp = mm_nt(v, o)
    m = jnp.max(s, axis=0, keepdims=True)
    e = jnp.exp(s - m)
    return [m, jnp.sum(e, axis=0, keepdims=True), jnp.sum(e * dp, axis=0, keepdims=True)]


def packed(quads):
    return jnp.concatenate(
        [jnp.concatenate([quads[i], quads[i + 2]], axis=0) for i in range(2)], axis=1
    )


def unpacked(tile, b):
    at = 4 * (b >> 1)
    return tile[at : at + KINDS, (b & 1) * PAIR : (b & 1) * PAIR + PAIR]


def near_stats_body(qo, kv, out):
    quads = []
    for b in range(SEG):
        rows = pl.ds(b * BLK, BLK)
        heads = [
            summary(qo[0, rows, head(h)], qo[1, rows, head(h)], kv[0, :, head(h)], kv[1, :, head(h)])
            for h in range(2)
        ]
        quads.append(
            jnp.concatenate(
                [jnp.concatenate([x, y], axis=1) for x, y in zip(*heads)]
                + [jnp.zeros((1, PAIR), F32)],
                axis=0,
            )
        )
    out[...] = packed(quads)


def near_stats(qo, kv):
    vm = pltpu.VMEM
    return call(
        near_stats_body,
        "near_stats",
        [((8, 2 * PAIR), F32, vm)],
        [vm, vm],
        [],
        2 * 2 * 2 * TOK * TOK * HD,
        1 << 20,
    )(qo, kv)[0]


def spread(value):
    lane = lax.broadcasted_iota(jnp.int32, (BLK, PAIR), 1)
    zero = jnp.zeros((BLK, PAIR), BF16)
    return jnp.concatenate(
        [jnp.where(lane < HD, value, zero), jnp.where(lane < HD, zero, value)], axis=0
    )


def load(pieces, sems):
    copies = [pltpu.make_async_copy(a, b, sems.at[i]) for i, (a, b) in enumerate(pieces)]
    for copy in copies:
        copy.start()

    def wait():
        for copy in copies:
            copy.wait()

    return wait


TILES = NX * ITEMS + UNROLL


def tile_copies(a, b, sems):
    def group(t):
        tiles = pl.ds(UNROLL * t, UNROLL)
        return pltpu.make_async_copy(a.at[tiles], b.at[tiles], sems.at[t])

    return group


def tile_sems():
    return pltpu.SemaphoreType.DMA((TILES // UNROLL,))


def each(count, act):
    def step(t, _):
        act(t)
        return 0

    lax.fori_loop(0, count, step, 0)


def queries(qos, block):
    n = jnp.minimum(block, NX * SEG - 1)
    rows = span(n & (SEG - 1))
    return spread(qos[n >> 2, 0, rows, :]), spread(qos[n >> 2, 1, rows, :])


def far_stats_body(
    listed, near, column_in, qos, out, high_out, e_out, dp_out,
    tally, column, e_keep, dp_keep, sems, e_sems, dp_sems,
):
    ready = load([(column_in.at[z], column.at[z]) for z in range(NZ)], sems)
    items = Listed(listed)
    e_sent = tile_copies(e_keep, e_out, e_sems)
    dp_sent = tile_copies(dp_keep, dp_out, dp_sems)
    kind = lax.broadcasted_iota(jnp.int32, (4, PAIR), 0)
    start = jnp.where(kind == 0, EMPTY, 0.0)
    for n in range(NX * SEG + 1):
        tally[n] = start
    ready()

    def group(t):
        numbers = [UNROLL * t + i for i in range(UNROLL)]
        found = []
        for n in numbers:
            place = items.place(n)
            cols = span(place & (SEG - 1))
            q, o = queries(qos, items.block(n))
            s = mm_nt(column[place >> 2, 0, cols, :], q) * SCALE
            dp = mm_nt(column[place >> 2, 1, cols, :], o)
            m = jnp.max(s, axis=0, keepdims=True)
            e = jnp.exp(s - m)
            found.append(
                (m, jnp.sum(e, axis=0, keepdims=True), jnp.sum(e * dp, axis=0, keepdims=True))
            )
            e_keep[n] = e.astype(BF16)
            dp_keep[n] = dp.astype(BF16)
            high_out[n] = jnp.broadcast_to(m, (8, PAIR))
        e_sent(t).start()
        dp_sent(t).start()
        for n, (m, l, t_sum) in zip(numbers, found):
            old = tally[items.block(n)]
            m0, l0, t0 = [old[i : i + 1, :] for i in range(KINDS)]
            high = jnp.maximum(m0, m)
            f0 = jnp.exp(m0 - high)
            f1 = jnp.exp(m - high)
            tally[items.block(n)] = jnp.concatenate(
                [high, l0 * f0 + l * f1, t0 * f0 + t_sum * f1, jnp.zeros_like(high)], axis=0
            )

    groups = (items.count + UNROLL - 1) // UNROLL
    each(groups, group)
    for d in range(NX):
        out[d] = packed([tally[d * SEG + b] for b in range(SEG)])
    out[NX] = near[...]
    each(groups, lambda t: e_sent(t).wait())
    each(groups, lambda t: dp_sent(t).wait())


def far_stats(listed, near, column, qos):
    vm = pltpu.VMEM
    tiles = (TILES, BLK, PAIR)
    return call(
        far_stats_body,
        "far_stats",
        [
            ((NX + 1, 8, 2 * PAIR), F32, vm),
            ((TILES, 8, PAIR), F32, vm),
            (tiles, BF16, pltpu.HBM),
            (tiles, BF16, pltpu.HBM),
        ],
        [pltpu.SMEM, vm, pltpu.HBM, vm],
        [
            vm((NX * SEG + 1, 4, PAIR), F32),
            vm((NZ, 2, TOK, PAIR), BF16),
            vm(tiles, BF16),
            vm(tiles, BF16),
            pltpu.SemaphoreType.DMA((NZ,)),
            tile_sems(),
            tile_sems(),
        ],
        2 * 2 * 2 * 16 * BLK * BLK * HD,
        6 << 20,
    )(listed, near, column, qos)


def joined(stats, my_x, x_q):
    parts = []
    for r in range(NX):
        x = (my_x - r) & (NX - 1)
        parts.append(stats[r, (x - x_q) & (NX - 1)])
    parts.append(stats[(my_x - x_q) & (NX - 1), NX])
    rows = []
    for at in (0, 4):
        high = functools.reduce(jnp.maximum, [p[at : at + 1, :] for p in parts])
        fade = [jnp.exp(p[at : at + 1, :] - high) for p in parts]
        total = sum(f * p[at + 1 : at + 2, :] for f, p in zip(fade, parts))
        mixed = sum(f * p[at + 2 : at + 3, :] for f, p in zip(fade, parts))
        inverse = 1.0 / total
        rows += [high, inverse, mixed * inverse, jnp.zeros_like(high)]
    return jnp.concatenate(rows, axis=0)


def weights_of(q, o, k, v, row):
    high, inverse, delta = [row[i : i + 1, :] for i in range(KINDS)]
    p = jnp.exp(mm_nt(k, q) * SCALE - high) * inverse
    ds = (p * (mm_nt(v, o) - delta) * SCALE).astype(BF16)
    return p.astype(BF16), ds


def far_grads_body(
    listed, me, stats, highs, e_in, dp_in, qos, kv_out, ds_out,
    total, rowed, staged, ds_keep, e_keep, dp_keep, out_sems, ds_sems, e_sems, dp_sems,
):
    my_x = me[0] >> 3
    items = Listed(listed)
    groups = (items.count + UNROLL - 1) // UNROLL
    sent = tile_copies(ds_keep, ds_out, ds_sems)
    e_got = tile_copies(e_in, e_keep, e_sems)
    dp_got = tile_copies(dp_in, dp_keep, dp_sems)

    def begin(t):
        e_got(t).start()
        dp_got(t).start()

    each(groups, begin)
    total[...] = jnp.zeros_like(total)
    for d in range(NX):
        tile = joined(stats, my_x, (my_x - d) & (NX - 1))
        for b in range(SEG):
            rowed[d * SEG + b, 0:KINDS, :] = unpacked(tile, b)
    rowed[NX * SEG] = jnp.zeros((8, PAIR), F32)

    def group(t):
        e_got(t).wait()
        dp_got(t).wait()
        numbers = [UNROLL * t + i for i in range(UNROLL)]
        found = []
        for n in numbers:
            row = rowed[items.block(n)]
            high, inverse, delta = [row[i : i + 1, :] for i in range(KINDS)]
            q, o = queries(qos, items.block(n))
            p = e_keep[n].astype(F32) * (jnp.exp(highs[n][0:1, :] - high) * inverse)
            ds = (p * (dp_keep[n].astype(F32) - delta) * SCALE).astype(BF16)
            found.append((ds, mm(ds, q), mm(p.astype(BF16), o)))
        for n, (ds, dk, dv) in zip(numbers, found):
            to = jnp.where(items.block(n) == NX * SEG, FAR, items.place(n))
            ds_keep[n] = ds
            total[to, 0] += dk
            total[to, 1] += dv
        sent(t).start()

    each(groups, group)
    copies = []
    for z in range(NZ):
        for s in range(2):
            for b in range(SEG):
                staged[z, pl.ds(s * TOK + b * BLK, BLK), :] = total[z * SEG + b, s].astype(BF16)
        copies.append(pltpu.make_async_copy(staged.at[z], kv_out.at[z], out_sems.at[z]))
        copies[-1].start()
    each(groups, lambda t: sent(t).wait())
    for copy in copies:
        copy.wait()


def far_grads(listed, me, stats, highs, e, dp, qos):
    vm = pltpu.VMEM
    tiles = (TILES, BLK, PAIR)
    return call(
        far_grads_body,
        "far_grads",
        [((NZ, 2 * TOK, PAIR), BF16, pltpu.HBM), (tiles, BF16, pltpu.HBM)],
        [pltpu.SMEM, pltpu.SMEM, vm, vm, pltpu.HBM, pltpu.HBM, vm],
        [
            vm((FAR + 1, 2, BLK, PAIR), F32),
            vm((NX * SEG + 1, 8, PAIR), F32),
            vm((NZ, 2 * TOK, PAIR), BF16),
            vm(tiles, BF16),
            vm(tiles, BF16),
            vm(tiles, BF16),
            pltpu.SemaphoreType.DMA((NZ,)),
            tile_sems(),
            tile_sems(),
            tile_sems(),
        ],
        4 * 2 * 2 * 16 * BLK * BLK * HD,
        12 << 20,
    )(listed, me, stats, highs, e, dp, qos)


def far_queries_body(listed, me, ds_in, column_in, dq_out, dq, ds_keep, keys, sems, ds_sems):
    ready = load([(column_in.at[z, 0], keys.at[z]) for z in range(NZ)], sems)
    my_x = me[0] >> 3
    items = Listed(listed)
    fetched = tile_copies(ds_in, ds_keep, ds_sems)
    groups = (items.count + UNROLL - 1) // UNROLL

    def begin(t, _):
        fetched(t).start()
        return 0

    lax.fori_loop(0, groups, begin, 0)
    dq[...] = jnp.zeros_like(dq)
    ready()

    def group(t, _):
        fetched(t).wait()
        numbers = [UNROLL * t + i for i in range(UNROLL)]
        found = []
        for n in numbers:
            place = items.place(n)
            k = keys[place >> 2, span(place & (SEG - 1)), :]
            ds = ds_keep[n]
            found.append(
                [mm_tn(ds[:, h * HD : h * HD + HD], k[:, h * HD : h * HD + HD]) for h in range(2)]
            )
        for n, heads in zip(numbers, found):
            for h in range(2):
                dq[items.block(n), :, head(h)] += heads[h]
        return 0

    lax.fori_loop(0, groups, group, 0)
    for d in range(NX):
        for b in range(SEG):
            dq_out[(my_x - d) & (NX - 1), pl.ds(b * BLK, BLK), :] = dq[d * SEG + b].astype(BF16)


def far_queries(listed, me, ds, column):
    vm = pltpu.VMEM
    tiles = NX * ITEMS + UNROLL
    return call(
        far_queries_body,
        "far_queries",
        [((NX, TOK, PAIR), BF16, vm)],
        [pltpu.SMEM, pltpu.SMEM, pltpu.HBM, pltpu.HBM],
        [
            vm((NX * SEG + 1, BLK, PAIR), F32),
            vm((tiles, BLK, PAIR), BF16),
            vm((NZ, TOK, PAIR), BF16),
            pltpu.SemaphoreType.DMA((NZ,)),
            pltpu.SemaphoreType.DMA((tiles // UNROLL,)),
        ],
        2 * 2 * 16 * BLK * BLK * HD,
        6 << 20,
    )(listed, me, ds, column)[0]


def interleave(out, rows, value):
    for h in range(2):
        rows[pl.ds(h, TOK, stride=2), :] = value[:, h * HD : h * HD + HD]
    out[...] = rows[...].astype(BF16)


def near_grads_body(me, stats, qo, kv, dq_far, dq_out, kv_out, p_keep, s_keep, dq, rows_keep):
    my_x = me[0] >> 3
    tile = joined(stats, my_x, my_x)
    for h in range(2):
        k = kv[0, :, head(h)]
        for b in range(SEG):
            rows = pl.ds(b * BLK, BLK)
            p, ds = weights_of(
                qo[0, rows, head(h)], qo[1, rows, head(h)], k, kv[1, :, head(h)],
                unpacked(tile, b)[:, h * HD : h * HD + HD],
            )
            part = mm_tn(ds, k)
            for x in range(NX):
                part = part + dq_far[x, rows, head(h)].astype(F32)
            dq[rows, head(h)] = part
            p_keep[:, rows] = p
            s_keep[:, rows] = ds
        kv_out[0, :, head(h)] = mm(s_keep[...], qo[0, :, head(h)])
        kv_out[1, :, head(h)] = mm(p_keep[...], qo[1, :, head(h)])
    interleave(dq_out, rows_keep, dq[...])


def near_grads(me, stats, qo, kv, dq_far):
    vm = pltpu.VMEM
    return call(
        near_grads_body,
        "near_grads",
        [((2 * TOK, HD), BF16, vm), ((2, TOK, PAIR), F32, vm)],
        [pltpu.SMEM] + [vm] * 4,
        [
            vm((TOK, TOK), BF16),
            vm((TOK, TOK), BF16),
            vm((TOK, PAIR), F32),
            vm((2 * TOK, HD), F32),
        ],
        5 * 2 * 2 * TOK * TOK * HD,
        4 << 20,
    )(me, stats, qo, kv, dq_far)


def finish_body(near, far, dk, dv, rows):
    for s, out in enumerate((dk, dv)):
        interleave(out, rows, near[s] + far[pl.ds(s * TOK, TOK), :].astype(F32))


def finish(near, far):
    vm = pltpu.VMEM
    return call(
        finish_body,
        "finish",
        [((2 * TOK, HD), BF16, vm)] * 2,
        [vm] * 2,
        [vm((2 * TOK, HD), F32)],
        0,
        2 << 20,
    )(near, far)


def by_head_body(first, second, out, rows):
    for s, ref in enumerate((first, second)):
        rows[...] = ref[...].astype(F32)
        for h in range(2):
            out[s, :, head(h)] = rows[pl.ds(h, TOK, stride=2), :].astype(BF16)


def by_head(first, second):
    vm = pltpu.VMEM
    return call(
        by_head_body,
        "by_head",
        [((2, TOK, PAIR), BF16, vm)],
        [vm] * 2,
        [vm((2 * TOK, HD), F32)],
        0,
        1 << 20,
    )(first.reshape(2 * TOK, HD), second.reshape(2 * TOK, HD))[0]


def triangle(lower):
    i = lax.broadcasted_iota(jnp.int32, (STRETCH, STRETCH), 0)
    j = lax.broadcasted_iota(jnp.int32, (STRETCH, STRETCH), 1)
    return i >= j if lower else i <= j


def head_map(transposed):
    shape = (WIDTH, SH) if transposed else (SH, WIDTH)
    wide = lax.broadcasted_iota(jnp.int32, shape, 0 if transposed else 1)
    head = lax.broadcasted_iota(jnp.int32, shape, 1 if transposed else 0)
    return ((wide >> 6) == head).astype(BF16)


def two_part(a, b):
    high = a.astype(BF16)
    low = (a - high.astype(F32)).astype(BF16)
    return mm(high, b) + mm(low, b)


def per_head(rates, state):
    return jnp.concatenate(
        [state[h * HP : (h + 1) * HP, :] * rates[0:1, h : h + 1] for h in range(SH)], axis=0
    )


def ends_body(x_ref, g_ref, ld_ref, b_ref, c_ref, ends, starts, pay):
    lower = triangle(True).astype(F32)
    spread = head_map(False)
    last = []
    for k in range(STRETCHES):
        rows = pl.ds(k * STRETCH, STRETCH)
        cumul = dot(lower, ld_ref[rows, :], ((1,), (0,)), HIGH)
        tot = cumul[STRETCH - 1 : STRETCH, :]
        last.append(tot)
        tail = two_part(jnp.exp(tot - cumul), spread)
        lead = two_part(jnp.exp(cumul), spread)
        x_in = (x_ref[rows, :].astype(F32) * tail).astype(BF16)
        g_in = (g_ref[rows, :].astype(F32) * lead).astype(BF16)
        ends[k] = mm_tn(x_in, b_ref[rows, :])
        starts[k] = mm_tn(g_in, c_ref[rows, :])
    rates = [jnp.exp(t) for t in last]
    state = ends[0]
    for k in range(1, STRETCHES):
        state = per_head(rates[k], state) + ends[k]
    pay[:, 0:ROWS, :] = state.astype(BF16).reshape(NS, ROWS, NST)
    grad = starts[STRETCHES - 1]
    for k in range(STRETCHES - 2, -1, -1):
        grad = per_head(rates[k], grad) + starts[k]
    pay[:, ROWS : 2 * ROWS, :] = grad.astype(BF16).reshape(NS, ROWS, NST)
    whole = functools.reduce(jnp.add, last)
    high = whole.astype(BF16).astype(F32)
    low = whole - high
    line = lax.broadcasted_iota(jnp.int32, (16, NST), 0)
    for r in range(NS):
        h = r // 2
        a = jnp.broadcast_to(high[0:1, h : h + 1], (16, NST))
        b = jnp.broadcast_to(low[0:1, h : h + 1], (16, NST))
        pay[r, 2 * ROWS : PAY, :] = jnp.where(
            line == 0, a, jnp.where(line == 1, b, 0.0)
        ).astype(BF16)


def scan_ends(x, g, ld, b, c):
    vm = pltpu.VMEM
    return call(
        ends_body,
        "scan_ends",
        [
            ((STRETCHES, WIDTH, NST), F32, vm),
            ((STRETCHES, WIDTH, NST), F32, vm),
            ((NS, PAY, NST), BF16, vm),
        ],
        [vm] * 5,
        [],
        2 * 2 * TOK * WIDTH * NST * 4,
        8 << 20,
    )(x, g, ld, b, c)


def prefix_body(inp, out):
    def forward(j, state):
        out[j, 0:ROWS, :] = state.astype(BF16)
        rest = inp[j, 2 * ROWS : PAY, :].astype(F32)
        rate = jnp.exp(rest[0:1, :] + rest[1:2, :])
        return rate * state + inp[j, 0:ROWS, :].astype(F32)

    def backward(t, grad):
        j = NS - 1 - t
        out[j, ROWS : 2 * ROWS, :] = grad.astype(BF16)
        rest = inp[j, 2 * ROWS : PAY, :].astype(F32)
        rate = jnp.exp(rest[0:1, :] + rest[1:2, :])
        return rate * grad + inp[j, ROWS : 2 * ROWS, :].astype(F32)

    zero = jnp.zeros((ROWS, NST), F32)
    lax.fori_loop(0, NS, forward, zero)
    lax.fori_loop(0, NS, backward, zero)


def scan_prefix(inp):
    vm = pltpu.VMEM
    return call(
        prefix_body,
        "scan_prefix",
        [((NS, 2 * ROWS, NST), BF16, vm)],
        [vm],
        [],
        0,
        2 << 20,
    )(inp)[0]


def grads_body(
    x_ref, g_ref, ld_ref, b_ref, c_ref, ends, starts, carried, dx_ref, dl_ref, bc_ref,
    states, grads, y_keep, d_keep,
):
    lower_mask = triangle(True)
    lower = lower_mask.astype(F32)
    upper = triangle(False).astype(F32)
    spread = head_map(False)
    gathered = head_map(True)
    ones = jnp.ones((8, NST), F32)
    rates = []
    for k in range(STRETCHES):
        ld = ld_ref[pl.ds(k * STRETCH, STRETCH), :]
        rates.append(jnp.exp(jnp.sum(ld, axis=0, keepdims=True)))
    state = carried[:, 0:ROWS, :].reshape(WIDTH, NST).astype(F32)
    states[0] = state.astype(BF16)
    for k in range(STRETCHES):
        state = per_head(rates[k], state) + ends[k]
        states[k + 1] = state.astype(BF16)
    grad = carried[:, ROWS : 2 * ROWS, :].reshape(WIDTH, NST).astype(F32)
    grads[STRETCHES - 1] = grad.astype(BF16)
    for k in range(STRETCHES - 1, 0, -1):
        grad = per_head(rates[k], grad) + starts[k]
        grads[k - 1] = grad.astype(BF16)

    def stretch(k, _):
        rows = pl.ds(pl.multiple_of(k * STRETCH, STRETCH), STRETCH)
        ld = ld_ref[rows, :]
        cumul = dot(lower, ld, ((1,), (0,)), HIGH)
        cumul_t = dot(ld, upper, ((0,), (0,)), HIGH)
        tot = cumul[STRETCH - 1 : STRETCH, :]
        b = b_ref[rows, :]
        c = c_ref[rows, :]
        cb = jnp.where(lower_mask, mm_nt(c, b), 0.0)
        mixed = jnp.zeros((STRETCH, STRETCH), F32)
        for h in range(SH):
            cols = pl.ds(h * HP, HP)
            x_h = x_ref[rows, cols]
            g_h = g_ref[rows, cols]
            gap = jnp.minimum(cumul[:, h : h + 1] - cumul_t[h : h + 1, :], 0.0)
            decay = jnp.exp(gap)
            weight = (decay * cb).astype(BF16)
            mixed = mixed + decay * mm_nt(g_h, x_h)
            y_keep[:, cols] = mm(weight, x_h)
            d_keep[:, cols] = mm_tn(weight, g_h)
        mixed = jnp.where(lower_mask, mixed, 0.0).astype(BF16)
        state = states[k]
        grad = grads[k]
        lead = two_part(jnp.exp(cumul), spread)
        tail = two_part(jnp.exp(tot - cumul), spread)
        x = x_ref[rows, :].astype(F32)
        g = g_ref[rows, :].astype(F32)
        y = y_keep[...] + lead * mm_nt(c, state)
        d = d_keep[...] + tail * mm_nt(b, grad)
        dx_ref[rows, :] = d.astype(BF16)
        bc_ref[rows, :] = (mm_tn(mixed, c) + mm((tail * x).astype(BF16), grad)).astype(BF16)
        c_rows = pl.ds(pl.multiple_of(TOK + k * STRETCH, STRETCH), STRETCH)
        bc_ref[c_rows, :] = (mm(mixed, b) + mm((lead * g).astype(BF16), state)).astype(BF16)
        change = two_part(g * y - x * d, gathered)
        meet = grad.astype(F32) * states[k + 1].astype(F32)
        meet = jnp.sum(meet.reshape(SH, HP, NST), axis=1)
        edge = dot(ones, meet, ((1,), (1,)), HIGH)[0:1, :]
        dl_ref[rows, :] = dot(upper, change, ((1,), (0,)), HIGH) + edge
        return 0

    lax.fori_loop(0, STRETCHES, stretch, 0)


def scan_grads(x, g, ld, b, c, ends, starts, carried):
    vm = pltpu.VMEM
    return call(
        grads_body,
        "scan_grads",
        [
            ((TOK, WIDTH), BF16, vm),
            ((TOK, SH), F32, vm),
            ((2 * TOK, NST), BF16, vm),
        ],
        [vm] * 8,
        [
            vm((STRETCHES + 1, WIDTH, NST), BF16),
            vm((STRETCHES, WIDTH, NST), BF16),
            vm((STRETCH, WIDTH), F32),
            vm((STRETCH, WIDTH), F32),
        ],
        2 * 8 * TOK * WIDTH * NST * 4,
        12 << 20,
    )(x, g, ld, b, c, ends, starts, carried)


def exchange(value, groups=None):
    return lax.all_to_all(value, "seq", 0, 0, tiled=True, axis_index_groups=groups)


def along_x(value, step):
    pairs = [
        (x * NZ + z, (x + step) % NX * NZ + z) for x in range(NX) for z in range(NZ)
    ]
    return lax.ppermute(value, "seq", pairs)


def after(value, *earlier):
    return lax.optimization_barrier((value, earlier))[0]


def per_device(q, k, v, o, x, ld, b, c, g, owner, offset, count):
    me = lax.axis_index("seq").astype(jnp.int32).reshape(1)
    kv = by_head(k, v)
    column = lax.all_gather(kv, "seq", axis_index_groups=Z_GROUPS)
    qo = by_head(q, o)
    live = jnp.arange(GLOB)[None, :] < count[:, None]
    codes = jnp.where(live, owner * SEG + offset, -1).reshape(NS * ITEMS)
    shifted = [along_x(qo, 1), along_x(qo, 3)]
    opposite = [along_x(shifted[0][:1], 1), along_x(shifted[1][1:], 3)]
    ends, starts, pay = scan_ends(x, g, ld, b, c)
    pay = exchange(after(pay, shifted[0], shifted[1]))
    listed = far_items(after(codes, pay), me)
    opposite = jnp.concatenate(after(opposite, pay))
    qos = jnp.stack([qo, shifted[0], opposite, shifted[1]])
    near = near_stats(after(qo, pay), kv)
    carried = exchange(scan_prefix(after(pay, near, listed, qos)))
    stats, highs, e_far, dp_far = far_stats(listed, near, column, qos)
    stats = jnp.stack([stats] + [along_x(stats, d) for d in range(1, NX)])
    kv_far, ds_far = far_grads(listed, me, stats, highs, e_far, dp_far, qos)
    kv_far = lax.psum_scatter(
        after(kv_far, carried), "seq", scatter_dimension=0, axis_index_groups=Z_GROUPS
    )
    dq_far = far_queries(listed, me, ds_far, column)
    dx, dl, bc = scan_grads(x, g, ld, b, c, ends, starts, carried)
    shares = lax.all_to_all(bc.reshape(8, 128, NST), "head", 0, 0, tiled=True)
    dq_far = exchange(after(dq_far, bc), X_GROUPS)
    part = jnp.sum(shares.astype(F32), axis=0).astype(BF16)
    whole = lax.all_gather(part, "head", tiled=True).astype(F32)
    dq, kv_near = near_grads(me, stats, qo, kv, dq_far)
    dk, dv = finish(kv_near, kv_far)
    return (
        dq.reshape(q.shape),
        dk.reshape(k.shape),
        dv.reshape(v.shape),
        dx,
        dl,
        whole[:TOK],
        whole[TOK:],
    )


def solution(mesh):
    wide = P("seq", "head", None)
    flat = P("seq", "head")
    own = P("seq", None)
    return jax.shard_map(
        per_device,
        mesh=mesh,
        in_specs=(wide, wide, wide, wide, flat, flat, own, own, flat, P(), P(), P()),
        out_specs=(wide, wide, wide, flat, flat, own, own),
        check_vma=False,
    )
```

```python
import functools
import math

import jax
import jax.numpy as jnp
from jax import lax
from jax.experimental import pallas as pl
from jax.experimental.pallas import tpu as pltpu
from jax.sharding import PartitionSpec as P

HD = 128
HP = 64
NST = 128
BLK = 128
STRETCH = 128
SEG = 4
GLOB = 4
TOK = 512
SH = 16
WIDTH = SH * HP
ITEMS = SEG * GLOB
NX = 4
NZ = 8
NS = NX * NZ
ROWS = WIDTH // NS
PAY = 2 * ROWS + 16
STRETCHES = TOK // STRETCH

HIGH = lax.Precision.HIGHEST
F32 = jnp.float32
BF16 = jnp.bfloat16
Z_GROUPS = [[x * NZ + z for z in range(NZ)] for x in range(NX)]
X_GROUPS = [[x * NZ + z for x in range(NX)] for z in range(NZ)]


def dot(a, b, dims, precision=None):
    return lax.dot_general(
        a, b, (dims, ((), ())), precision=precision, preferred_element_type=F32
    )


def mm(a, b):
    return dot(a, b, ((1,), (0,)))


def mm_nt(a, b):
    return dot(a, b, ((1,), (1,)))


def mm_tn(a, b):
    return dot(a, b, ((0,), (0,)))


def call(body, name, outs, ins, scratch, flops, nbytes, vmem=48 << 20):
    return pl.pallas_call(
        body,
        out_shape=[jax.ShapeDtypeStruct(s, d) for s, d, _ in outs],
        in_specs=[pl.BlockSpec(memory_space=m) for m in ins],
        out_specs=[pl.BlockSpec(memory_space=m) for _, _, m in outs],
        scratch_shapes=scratch,
        compiler_params=pltpu.CompilerParams(vmem_limit_bytes=vmem),
        cost_estimate=pl.CostEstimate(flops=flops, bytes_accessed=nbytes, transcendentals=0),
        name=name,
    )


SCALE = 1.0 / math.sqrt(HD)
EMPTY = -1e30
KINDS = 3
FAR = NZ * SEG
UNROLL = 8
PAIR = 2 * HD


def far_items(codes, me):
    my_x = me[0] >> 3
    my_z = me[0] & (NZ - 1)
    sources = ((my_x - jnp.arange(NX)) & (NX - 1)) * NZ + my_z
    code = jnp.take(codes.reshape(NS, ITEMS), sources, axis=0).reshape(NX * ITEMS)
    block = jnp.arange(NX * ITEMS) // GLOB
    hit = (code >= 0) & ((code >> 5) == my_x)
    order = jnp.arange(NX * ITEMS)
    rank = jnp.sum((hit[None, :] & (order[None, :] < order[:, None])).astype(jnp.int32), axis=1)
    slot = jnp.arange(NX * ITEMS + UNROLL)[:, None]
    chosen = hit[None, :] & (rank[None, :] == slot)
    places = jnp.sum(jnp.where(chosen, code[None, :] & (FAR - 1), 0), axis=1)
    blocks = NX * SEG + jnp.sum(jnp.where(chosen, block[None, :] - NX * SEG, 0), axis=1)
    count = jnp.sum(hit.astype(jnp.int32)).reshape(1)
    return jnp.concatenate([count, places, blocks]).astype(jnp.int32)


class Listed:
    def __init__(self, ref):
        self.count = ref[0]
        self.place = lambda n: ref[1 + n]
        self.block = lambda n: ref[1 + NX * ITEMS + UNROLL + n]


def span(index):
    return pl.ds(pl.multiple_of(index * BLK, BLK), BLK)


def in_groups(count, visit):
    def group(t, _):
        visit([UNROLL * t + i for i in range(UNROLL)])
        return 0

    lax.fori_loop(0, (count + UNROLL - 1) // UNROLL, group, 0)


def head(h):
    return pl.ds(h * HD, HD)


def summary(q, o, k, v):
    s = mm_nt(k, q) * SCALE
    dp = mm_nt(v, o)
    m = jnp.max(s, axis=0, keepdims=True)
    e = jnp.exp(s - m)
    return [m, jnp.sum(e, axis=0, keepdims=True), jnp.sum(e * dp, axis=0, keepdims=True)]


def packed(quads):
    return jnp.concatenate(
        [jnp.concatenate([quads[i], quads[i + 2]], axis=0) for i in range(2)], axis=1
    )


def unpacked(tile, b):
    at = 4 * (b >> 1)
    return tile[at : at + KINDS, (b & 1) * PAIR : (b & 1) * PAIR + PAIR]


def near_stats_body(qo, kv, out):
    quads = []
    for b in range(SEG):
        rows = pl.ds(b * BLK, BLK)
        heads = [
            summary(qo[0, rows, head(h)], qo[1, rows, head(h)], kv[0, :, head(h)], kv[1, :, head(h)])
            for h in range(2)
        ]
        quads.append(
            jnp.concatenate(
                [jnp.concatenate([x, y], axis=1) for x, y in zip(*heads)]
                + [jnp.zeros((1, PAIR), F32)],
                axis=0,
            )
        )
    out[...] = packed(quads)


def near_stats(qo, kv):
    vm = pltpu.VMEM
    return call(
        near_stats_body,
        "near_stats",
        [((8, 2 * PAIR), F32, vm)],
        [vm, vm],
        [],
        2 * 2 * 2 * TOK * TOK * HD,
        1 << 20,
    )(qo, kv)[0]


def spread(value):
    lane = lax.broadcasted_iota(jnp.int32, (BLK, PAIR), 1)
    zero = jnp.zeros((BLK, PAIR), BF16)
    return jnp.concatenate(
        [jnp.where(lane < HD, value, zero), jnp.where(lane < HD, zero, value)], axis=0
    )


def load(pieces, sems):
    copies = [pltpu.make_async_copy(a, b, sems.at[i]) for i, (a, b) in enumerate(pieces)]
    for copy in copies:
        copy.start()

    def wait():
        for copy in copies:
            copy.wait()

    return wait


TILES = NX * ITEMS + UNROLL


def tile_copies(a, b, sems):
    def group(t):
        tiles = pl.ds(UNROLL * t, UNROLL)
        return pltpu.make_async_copy(a.at[tiles], b.at[tiles], sems.at[t])

    return group


def tile_sems():
    return pltpu.SemaphoreType.DMA((TILES // UNROLL,))


def each(count, act):
    def step(t, _):
        act(t)
        return 0

    lax.fori_loop(0, count, step, 0)


def queries(qos, block):
    n = jnp.minimum(block, NX * SEG - 1)
    rows = span(n & (SEG - 1))
    return spread(qos[n >> 2, 0, rows, :]), spread(qos[n >> 2, 1, rows, :])


def far_stats_body(
    listed, near, column_in, qos, out, high_out, e_out, dp_out,
    tally, column, e_keep, dp_keep, sems, e_sems, dp_sems,
):
    ready = load([(column_in.at[z], column.at[z]) for z in range(NZ)], sems)
    items = Listed(listed)
    e_sent = tile_copies(e_keep, e_out, e_sems)
    dp_sent = tile_copies(dp_keep, dp_out, dp_sems)
    kind = lax.broadcasted_iota(jnp.int32, (4, PAIR), 0)
    start = jnp.where(kind == 0, EMPTY, 0.0)
    for n in range(NX * SEG + 1):
        tally[n] = start
    ready()

    def group(t):
        numbers = [UNROLL * t + i for i in range(UNROLL)]
        found = []
        for n in numbers:
            place = items.place(n)
            cols = span(place & (SEG - 1))
            q, o = queries(qos, items.block(n))
            s = mm_nt(column[place >> 2, 0, cols, :], q) * SCALE
            dp = mm_nt(column[place >> 2, 1, cols, :], o)
            m = jnp.max(s, axis=0, keepdims=True)
            e = jnp.exp(s - m)
            found.append(
                (m, jnp.sum(e, axis=0, keepdims=True), jnp.sum(e * dp, axis=0, keepdims=True))
            )
            e_keep[n] = e.astype(BF16)
            dp_keep[n] = dp.astype(BF16)
            high_out[n] = jnp.broadcast_to(m, (8, PAIR))
        e_sent(t).start()
        dp_sent(t).start()
        for n, (m, l, t_sum) in zip(numbers, found):
            old = tally[items.block(n)]
            m0, l0, t0 = [old[i : i + 1, :] for i in range(KINDS)]
            high = jnp.maximum(m0, m)
            f0 = jnp.exp(m0 - high)
            f1 = jnp.exp(m - high)
            tally[items.block(n)] = jnp.concatenate(
                [high, l0 * f0 + l * f1, t0 * f0 + t_sum * f1, jnp.zeros_like(high)], axis=0
            )

    groups = (items.count + UNROLL - 1) // UNROLL
    each(groups, group)
    for d in range(NX):
        out[d] = packed([tally[d * SEG + b] for b in range(SEG)])
    out[NX] = near[...]
    each(groups, lambda t: e_sent(t).wait())
    each(groups, lambda t: dp_sent(t).wait())


def far_stats(listed, near, column, qos):
    vm = pltpu.VMEM
    tiles = (TILES, BLK, PAIR)
    return call(
        far_stats_body,
        "far_stats",
        [
            ((NX + 1, 8, 2 * PAIR), F32, vm),
            ((TILES, 8, PAIR), F32, vm),
            (tiles, BF16, pltpu.HBM),
            (tiles, BF16, pltpu.HBM),
        ],
        [pltpu.SMEM, vm, pltpu.HBM, vm],
        [
            vm((NX * SEG + 1, 4, PAIR), F32),
            vm((NZ, 2, TOK, PAIR), BF16),
            vm(tiles, BF16),
            vm(tiles, BF16),
            pltpu.SemaphoreType.DMA((NZ,)),
            tile_sems(),
            tile_sems(),
        ],
        2 * 2 * 2 * 16 * BLK * BLK * HD,
        6 << 20,
    )(listed, near, column, qos)


def joined(stats, my_x, x_q):
    parts = []
    for r in range(NX):
        x = (my_x - r) & (NX - 1)
        parts.append(stats[r, (x - x_q) & (NX - 1)])
    parts.append(stats[(my_x - x_q) & (NX - 1), NX])
    rows = []
    for at in (0, 4):
        high = functools.reduce(jnp.maximum, [p[at : at + 1, :] for p in parts])
        fade = [jnp.exp(p[at : at + 1, :] - high) for p in parts]
        total = sum(f * p[at + 1 : at + 2, :] for f, p in zip(fade, parts))
        mixed = sum(f * p[at + 2 : at + 3, :] for f, p in zip(fade, parts))
        inverse = 1.0 / total
        rows += [high, inverse, mixed * inverse, jnp.zeros_like(high)]
    return jnp.concatenate(rows, axis=0)


def weights_of(q, o, k, v, row):
    high, inverse, delta = [row[i : i + 1, :] for i in range(KINDS)]
    p = jnp.exp(mm_nt(k, q) * SCALE - high) * inverse
    ds = (p * (mm_nt(v, o) - delta) * SCALE).astype(BF16)
    return p.astype(BF16), ds


def far_grads_body(
    listed, me, stats, highs, e_in, dp_in, qos, kv_out, ds_out,
    total, rowed, staged, ds_keep, e_keep, dp_keep, out_sems, ds_sems, e_sems, dp_sems,
):
    my_x = me[0] >> 3
    items = Listed(listed)
    groups = (items.count + UNROLL - 1) // UNROLL
    sent = tile_copies(ds_keep, ds_out, ds_sems)
    e_got = tile_copies(e_in, e_keep, e_sems)
    dp_got = tile_copies(dp_in, dp_keep, dp_sems)

    def begin(t):
        e_got(t).start()
        dp_got(t).start()

    each(groups, begin)
    total[...] = jnp.zeros_like(total)
    for d in range(NX):
        tile = joined(stats, my_x, (my_x - d) & (NX - 1))
        for b in range(SEG):
            rowed[d * SEG + b, 0:KINDS, :] = unpacked(tile, b)
    rowed[NX * SEG] = jnp.zeros((8, PAIR), F32)

    def group(t):
        e_got(t).wait()
        dp_got(t).wait()
        numbers = [UNROLL * t + i for i in range(UNROLL)]
        found = []
        for n in numbers:
            row = rowed[items.block(n)]
            high, inverse, delta = [row[i : i + 1, :] for i in range(KINDS)]
            q, o = queries(qos, items.block(n))
            p = e_keep[n].astype(F32) * (jnp.exp(highs[n][0:1, :] - high) * inverse)
            ds = (p * (dp_keep[n].astype(F32) - delta) * SCALE).astype(BF16)
            found.append((ds, mm(ds, q), mm(p.astype(BF16), o)))
        for n, (ds, dk, dv) in zip(numbers, found):
            to = jnp.where(items.block(n) == NX * SEG, FAR, items.place(n))
            ds_keep[n] = ds
            total[to, 0] += dk
            total[to, 1] += dv
        sent(t).start()

    each(groups, group)
    copies = []
    for z in range(NZ):
        for s in range(2):
            for b in range(SEG):
                staged[z, pl.ds(s * TOK + b * BLK, BLK), :] = total[z * SEG + b, s].astype(BF16)
        copies.append(pltpu.make_async_copy(staged.at[z], kv_out.at[z], out_sems.at[z]))
        copies[-1].start()
    each(groups, lambda t: sent(t).wait())
    for copy in copies:
        copy.wait()


def far_grads(listed, me, stats, highs, e, dp, qos):
    vm = pltpu.VMEM
    tiles = (TILES, BLK, PAIR)
    return call(
        far_grads_body,
        "far_grads",
        [((NZ, 2 * TOK, PAIR), BF16, pltpu.HBM), (tiles, BF16, pltpu.HBM)],
        [pltpu.SMEM, pltpu.SMEM, vm, vm, pltpu.HBM, pltpu.HBM, vm],
        [
            vm((FAR + 1, 2, BLK, PAIR), F32),
            vm((NX * SEG + 1, 8, PAIR), F32),
            vm((NZ, 2 * TOK, PAIR), BF16),
            vm(tiles, BF16),
            vm(tiles, BF16),
            vm(tiles, BF16),
            pltpu.SemaphoreType.DMA((NZ,)),
            tile_sems(),
            tile_sems(),
            tile_sems(),
        ],
        4 * 2 * 2 * 16 * BLK * BLK * HD,
        12 << 20,
    )(listed, me, stats, highs, e, dp, qos)


def far_queries_body(listed, me, ds_in, column_in, dq_out, dq, ds_keep, keys, sems, ds_sems):
    ready = load([(column_in.at[z, 0], keys.at[z]) for z in range(NZ)], sems)
    my_x = me[0] >> 3
    items = Listed(listed)
    fetched = tile_copies(ds_in, ds_keep, ds_sems)
    groups = (items.count + UNROLL - 1) // UNROLL

    def begin(t, _):
        fetched(t).start()
        return 0

    lax.fori_loop(0, groups, begin, 0)
    dq[...] = jnp.zeros_like(dq)
    ready()

    def group(t, _):
        fetched(t).wait()
        numbers = [UNROLL * t + i for i in range(UNROLL)]
        found = []
        for n in numbers:
            place = items.place(n)
            k = keys[place >> 2, span(place & (SEG - 1)), :]
            ds = ds_keep[n]
            found.append(
                [mm_tn(ds[:, h * HD : h * HD + HD], k[:, h * HD : h * HD + HD]) for h in range(2)]
            )
        for n, heads in zip(numbers, found):
            for h in range(2):
                dq[items.block(n), :, head(h)] += heads[h]
        return 0

    lax.fori_loop(0, groups, group, 0)
    for d in range(NX):
        for b in range(SEG):
            dq_out[(my_x - d) & (NX - 1), pl.ds(b * BLK, BLK), :] = dq[d * SEG + b].astype(BF16)


def far_queries(listed, me, ds, column):
    vm = pltpu.VMEM
    tiles = NX * ITEMS + UNROLL
    return call(
        far_queries_body,
        "far_queries",
        [((NX, TOK, PAIR), BF16, vm)],
        [pltpu.SMEM, pltpu.SMEM, pltpu.HBM, pltpu.HBM],
        [
            vm((NX * SEG + 1, BLK, PAIR), F32),
            vm((tiles, BLK, PAIR), BF16),
            vm((NZ, TOK, PAIR), BF16),
            pltpu.SemaphoreType.DMA((NZ,)),
            pltpu.SemaphoreType.DMA((tiles // UNROLL,)),
        ],
        2 * 2 * 16 * BLK * BLK * HD,
        6 << 20,
    )(listed, me, ds, column)[0]


def interleave(out, rows, value):
    for h in range(2):
        rows[pl.ds(h, TOK, stride=2), :] = value[:, h * HD : h * HD + HD]
    out[...] = rows[...].astype(BF16)


def near_grads_body(me, stats, qo, kv, dq_far, dq_out, kv_out, p_keep, s_keep, dq, rows_keep):
    my_x = me[0] >> 3
    tile = joined(stats, my_x, my_x)
    for h in range(2):
        k = kv[0, :, head(h)]
        for b in range(SEG):
            rows = pl.ds(b * BLK, BLK)
            p, ds = weights_of(
                qo[0, rows, head(h)], qo[1, rows, head(h)], k, kv[1, :, head(h)],
                unpacked(tile, b)[:, h * HD : h * HD + HD],
            )
            part = mm_tn(ds, k)
            for x in range(NX):
                part = part + dq_far[x, rows, head(h)].astype(F32)
            dq[rows, head(h)] = part
            p_keep[:, rows] = p
            s_keep[:, rows] = ds
        kv_out[0, :, head(h)] = mm(s_keep[...], qo[0, :, head(h)])
        kv_out[1, :, head(h)] = mm(p_keep[...], qo[1, :, head(h)])
    interleave(dq_out, rows_keep, dq[...])


def near_grads(me, stats, qo, kv, dq_far):
    vm = pltpu.VMEM
    return call(
        near_grads_body,
        "near_grads",
        [((2 * TOK, HD), BF16, vm), ((2, TOK, PAIR), F32, vm)],
        [pltpu.SMEM] + [vm] * 4,
        [
            vm((TOK, TOK), BF16),
            vm((TOK, TOK), BF16),
            vm((TOK, PAIR), F32),
            vm((2 * TOK, HD), F32),
        ],
        5 * 2 * 2 * TOK * TOK * HD,
        4 << 20,
    )(me, stats, qo, kv, dq_far)


def finish_body(near, far, dk, dv, rows):
    for s, out in enumerate((dk, dv)):
        interleave(out, rows, near[s] + far[pl.ds(s * TOK, TOK), :].astype(F32))


def finish(near, far):
    vm = pltpu.VMEM
    return call(
        finish_body,
        "finish",
        [((2 * TOK, HD), BF16, vm)] * 2,
        [vm] * 2,
        [vm((2 * TOK, HD), F32)],
        0,
        2 << 20,
    )(near, far)


def by_head_body(first, second, out, rows):
    for s, ref in enumerate((first, second)):
        rows[...] = ref[...].astype(F32)
        for h in range(2):
            out[s, :, head(h)] = rows[pl.ds(h, TOK, stride=2), :].astype(BF16)


def by_head(first, second):
    vm = pltpu.VMEM
    return call(
        by_head_body,
        "by_head",
        [((2, TOK, PAIR), BF16, vm)],
        [vm] * 2,
        [vm((2 * TOK, HD), F32)],
        0,
        1 << 20,
    )(first.reshape(2 * TOK, HD), second.reshape(2 * TOK, HD))[0]


def triangle(lower):
    i = lax.broadcasted_iota(jnp.int32, (STRETCH, STRETCH), 0)
    j = lax.broadcasted_iota(jnp.int32, (STRETCH, STRETCH), 1)
    return i >= j if lower else i <= j


def head_map(transposed):
    shape = (WIDTH, SH) if transposed else (SH, WIDTH)
    wide = lax.broadcasted_iota(jnp.int32, shape, 0 if transposed else 1)
    head = lax.broadcasted_iota(jnp.int32, shape, 1 if transposed else 0)
    return ((wide >> 6) == head).astype(BF16)


def two_part(a, b):
    high = a.astype(BF16)
    low = (a - high.astype(F32)).astype(BF16)
    return mm(high, b) + mm(low, b)


def per_head(rates, state):
    return jnp.concatenate(
        [state[h * HP : (h + 1) * HP, :] * rates[0:1, h : h + 1] for h in range(SH)], axis=0
    )


def ends_body(x_ref, g_ref, ld_ref, b_ref, c_ref, ends, starts, pay):
    lower = triangle(True).astype(F32)
    spread = head_map(False)
    last = []
    for k in range(STRETCHES):
        rows = pl.ds(k * STRETCH, STRETCH)
        cumul = dot(lower, ld_ref[rows, :], ((1,), (0,)), HIGH)
        tot = cumul[STRETCH - 1 : STRETCH, :]
        last.append(tot)
        tail = two_part(jnp.exp(tot - cumul), spread)
        lead = two_part(jnp.exp(cumul), spread)
        x_in = (x_ref[rows, :].astype(F32) * tail).astype(BF16)
        g_in = (g_ref[rows, :].astype(F32) * lead).astype(BF16)
        ends[k] = mm_tn(x_in, b_ref[rows, :])
        starts[k] = mm_tn(g_in, c_ref[rows, :])
    rates = [jnp.exp(t) for t in last]
    state = ends[0]
    for k in range(1, STRETCHES):
        state = per_head(rates[k], state) + ends[k]
    pay[:, 0:ROWS, :] = state.astype(BF16).reshape(NS, ROWS, NST)
    grad = starts[STRETCHES - 1]
    for k in range(STRETCHES - 2, -1, -1):
        grad = per_head(rates[k], grad) + starts[k]
    pay[:, ROWS : 2 * ROWS, :] = grad.astype(BF16).reshape(NS, ROWS, NST)
    whole = functools.reduce(jnp.add, last)
    high = whole.astype(BF16).astype(F32)
    low = whole - high
    line = lax.broadcasted_iota(jnp.int32, (16, NST), 0)
    for r in range(NS):
        h = r // 2
        a = jnp.broadcast_to(high[0:1, h : h + 1], (16, NST))
        b = jnp.broadcast_to(low[0:1, h : h + 1], (16, NST))
        pay[r, 2 * ROWS : PAY, :] = jnp.where(
            line == 0, a, jnp.where(line == 1, b, 0.0)
        ).astype(BF16)


def scan_ends(x, g, ld, b, c):
    vm = pltpu.VMEM
    return call(
        ends_body,
        "scan_ends",
        [
            ((STRETCHES, WIDTH, NST), F32, vm),
            ((STRETCHES, WIDTH, NST), F32, vm),
            ((NS, PAY, NST), BF16, vm),
        ],
        [vm] * 5,
        [],
        2 * 2 * TOK * WIDTH * NST * 4,
        8 << 20,
    )(x, g, ld, b, c)


def prefix_body(inp, out):
    def forward(j, state):
        out[j, 0:ROWS, :] = state.astype(BF16)
        rest = inp[j, 2 * ROWS : PAY, :].astype(F32)
        rate = jnp.exp(rest[0:1, :] + rest[1:2, :])
        return rate * state + inp[j, 0:ROWS, :].astype(F32)

    def backward(t, grad):
        j = NS - 1 - t
        out[j, ROWS : 2 * ROWS, :] = grad.astype(BF16)
        rest = inp[j, 2 * ROWS : PAY, :].astype(F32)
        rate = jnp.exp(rest[0:1, :] + rest[1:2, :])
        return rate * grad + inp[j, ROWS : 2 * ROWS, :].astype(F32)

    zero = jnp.zeros((ROWS, NST), F32)
    lax.fori_loop(0, NS, forward, zero)
    lax.fori_loop(0, NS, backward, zero)


def scan_prefix(inp):
    vm = pltpu.VMEM
    return call(
        prefix_body,
        "scan_prefix",
        [((NS, 2 * ROWS, NST), BF16, vm)],
        [vm],
        [],
        0,
        2 << 20,
    )(inp)[0]


def grads_body(
    x_ref, g_ref, ld_ref, b_ref, c_ref, ends, starts, carried, dx_ref, dl_ref, bc_ref,
    states, grads, y_keep, d_keep,
):
    lower_mask = triangle(True)
    lower = lower_mask.astype(F32)
    upper = triangle(False).astype(F32)
    spread = head_map(False)
    gathered = head_map(True)
    ones = jnp.ones((8, NST), F32)
    rates = []
    for k in range(STRETCHES):
        ld = ld_ref[pl.ds(k * STRETCH, STRETCH), :]
        rates.append(jnp.exp(jnp.sum(ld, axis=0, keepdims=True)))
    state = carried[:, 0:ROWS, :].reshape(WIDTH, NST).astype(F32)
    states[0] = state.astype(BF16)
    for k in range(STRETCHES):
        state = per_head(rates[k], state) + ends[k]
        states[k + 1] = state.astype(BF16)
    grad = carried[:, ROWS : 2 * ROWS, :].reshape(WIDTH, NST).astype(F32)
    grads[STRETCHES - 1] = grad.astype(BF16)
    for k in range(STRETCHES - 1, 0, -1):
        grad = per_head(rates[k], grad) + starts[k]
        grads[k - 1] = grad.astype(BF16)

    def stretch(k, _):
        rows = pl.ds(pl.multiple_of(k * STRETCH, STRETCH), STRETCH)
        ld = ld_ref[rows, :]
        cumul = dot(lower, ld, ((1,), (0,)), HIGH)
        cumul_t = dot(ld, upper, ((0,), (0,)), HIGH)
        tot = cumul[STRETCH - 1 : STRETCH, :]
        b = b_ref[rows, :]
        c = c_ref[rows, :]
        cb = jnp.where(lower_mask, mm_nt(c, b), 0.0)
        mixed = jnp.zeros((STRETCH, STRETCH), F32)
        for h in range(SH):
            cols = pl.ds(h * HP, HP)
            x_h = x_ref[rows, cols]
            g_h = g_ref[rows, cols]
            gap = jnp.minimum(cumul[:, h : h + 1] - cumul_t[h : h + 1, :], 0.0)
            decay = jnp.exp(gap)
            weight = (decay * cb).astype(BF16)
            mixed = mixed + decay * mm_nt(g_h, x_h)
            y_keep[:, cols] = mm(weight, x_h)
            d_keep[:, cols] = mm_tn(weight, g_h)
        mixed = jnp.where(lower_mask, mixed, 0.0).astype(BF16)
        state = states[k]
        grad = grads[k]
        lead = two_part(jnp.exp(cumul), spread)
        tail = two_part(jnp.exp(tot - cumul), spread)
        x = x_ref[rows, :].astype(F32)
        g = g_ref[rows, :].astype(F32)
        y = y_keep[...] + lead * mm_nt(c, state)
        d = d_keep[...] + tail * mm_nt(b, grad)
        dx_ref[rows, :] = d.astype(BF16)
        bc_ref[rows, :] = (mm_tn(mixed, c) + mm((tail * x).astype(BF16), grad)).astype(BF16)
        c_rows = pl.ds(pl.multiple_of(TOK + k * STRETCH, STRETCH), STRETCH)
        bc_ref[c_rows, :] = (mm(mixed, b) + mm((lead * g).astype(BF16), state)).astype(BF16)
        change = two_part(g * y - x * d, gathered)
        meet = grad.astype(F32) * states[k + 1].astype(F32)
        meet = jnp.sum(meet.reshape(SH, HP, NST), axis=1)
        edge = dot(ones, meet, ((1,), (1,)), HIGH)[0:1, :]
        dl_ref[rows, :] = dot(upper, change, ((1,), (0,)), HIGH) + edge
        return 0

    lax.fori_loop(0, STRETCHES, stretch, 0)


def scan_grads(x, g, ld, b, c, ends, starts, carried):
    vm = pltpu.VMEM
    return call(
        grads_body,
        "scan_grads",
        [
            ((TOK, WIDTH), BF16, vm),
            ((TOK, SH), F32, vm),
            ((2 * TOK, NST), BF16, vm),
        ],
        [vm] * 8,
        [
            vm((STRETCHES + 1, WIDTH, NST), BF16),
            vm((STRETCHES, WIDTH, NST), BF16),
            vm((STRETCH, WIDTH), F32),
            vm((STRETCH, WIDTH), F32),
        ],
        2 * 8 * TOK * WIDTH * NST * 4,
        12 << 20,
    )(x, g, ld, b, c, ends, starts, carried)


def exchange(value, groups=None):
    return lax.all_to_all(value, "seq", 0, 0, tiled=True, axis_index_groups=groups)


def along_x(value, step):
    pairs = [
        (x * NZ + z, (x + step) % NX * NZ + z) for x in range(NX) for z in range(NZ)
    ]
    return lax.ppermute(value, "seq", pairs)


def after(value, *earlier):
    return lax.optimization_barrier((value, earlier))[0]


def per_device(q, k, v, o, x, ld, b, c, g, owner, offset, count):
    me = lax.axis_index("seq").astype(jnp.int32).reshape(1)
    kv = by_head(k, v)
    column = lax.all_gather(kv, "seq", axis_index_groups=Z_GROUPS)
    qo = by_head(q, o)
    live = jnp.arange(GLOB)[None, :] < count[:, None]
    codes = jnp.where(live, owner * SEG + offset, -1).reshape(NS * ITEMS)
    shifted = [along_x(qo, 1), along_x(qo, 3)]
    opposite = [along_x(shifted[0][:1], 1), along_x(shifted[1][1:], 3)]
    ends, starts, pay = scan_ends(x, g, ld, b, c)
    pay = exchange(after(pay, shifted[0], shifted[1]))
    listed = far_items(after(codes, pay), me)
    opposite = jnp.concatenate(after(opposite, pay))
    qos = jnp.stack([qo, shifted[0], opposite, shifted[1]])
    near = near_stats(after(qo, pay), kv)
    carried = exchange(scan_prefix(after(pay, near, listed, qos)))
    stats, highs, e_far, dp_far = far_stats(listed, near, column, qos)
    stats = jnp.stack([stats] + [along_x(stats, d) for d in range(1, NX)])
    kv_far, ds_far = far_grads(listed, me, stats, highs, e_far, dp_far, qos)
    kv_far = lax.psum_scatter(
        after(kv_far, carried), "seq", scatter_dimension=0, axis_index_groups=Z_GROUPS
    )
    dq_far = far_queries(listed, me, ds_far, column)
    dx, dl, bc = scan_grads(x, g, ld, b, c, ends, starts, carried)
    shares = lax.all_to_all(bc.reshape(8, 128, NST), "head", 0, 0, tiled=True)
    dq_far = exchange(after(dq_far, bc), X_GROUPS)
    part = jnp.sum(shares.astype(F32), axis=0).astype(BF16)
    whole = lax.all_gather(part, "head", tiled=True).astype(F32)
    dq, kv_near = near_grads(me, stats, qo, kv, dq_far)
    dk, dv = finish(kv_near, kv_far)
    return (
        dq.reshape(q.shape),
        dk.reshape(k.shape),
        dv.reshape(v.shape),
        dx,
        dl,
        whole[:TOK],
        whole[TOK:],
    )


def solution(mesh):
    wide = P("seq", "head", None)
    flat = P("seq", "head")
    own = P("seq", None)
    return jax.shard_map(
        per_device,
        mesh=mesh,
        in_specs=(wide, wide, wide, wide, flat, flat, own, own, flat, P(), P(), P()),
        out_specs=(wide, wide, wide, flat, flat, own, own),
        check_vma=False,
    )
```
